512 devices in a mesh: ctx: 128 (over z, y, core), head: 4 (over x).
Axes of the slice: x: 4, y: 4, z: 16, core: 2. Of those that a mesh axis runs over, the one named last changes fastest.
Arguments:
- queries: bfloat16 [16384, 4096], P(('ctx', 'head')), may hold values from -24 to 24
- key_rows: bfloat16 [16384, 4096], P(('ctx', 'head')), may hold values from -12 to 12
- value_rows: bfloat16 [16384, 4096], P(('ctx', 'head')), may hold values from -6 to 6
- rel_bias: float32 [32, 32], P(None, 'head'), may hold values from -4 to 4
- offsets: int32 [2, 32], P(None, 'head'), may hold values from 0 to 63, as said below
Outputs:
- attended: bfloat16 [16384, 4096], P(('ctx', 'head'))
The draws below stay inside these ranges and needn't reach their ends.
Inputs may be any that keep to these rules, and one draw needn't show every extreme that they name: offsets[0, h] is below 4 and offsets[1, h] is below 64.
All inputs are finite; a program needn't handle non-finite values.
Results may differ from the reference program's by a relative error of at most 0.005.
Values may be sent and summed in bfloat16 or wider, within the bound.
No kernel may reach another device: no remote copies, remote signals or barrier semaphores. Data moves between devices by JAX's collectives and lax.ppermute only.
A program may use at most 64 MiB of HBM per device.

```python
import math
import jax
import jax.numpy as jnp
from jax import lax

HEADS = 32
DH = 128
WIDTH = 4096
BUCKETS = 32
MAXDIST = 128
R1 = 4
SPAN = 256
TOKENS = 16384
R2 = 64


def draw_queries(key, part):
    drawn = jnp.clip(1.5 * jax.random.normal(jax.random.fold_in(key, 1), (TOKENS, WIDTH), jnp.float32), -6.0, 6.0)
    return drawn.astype(jnp.bfloat16)


def draw_key_rows(key, part):
    drawn = jnp.clip(jax.random.normal(jax.random.fold_in(key, 2), (TOKENS, WIDTH), jnp.float32), -4.0, 4.0)
    return drawn.astype(jnp.bfloat16)


def draw_offsets(key, part):
    base = jax.random.fold_in(key, 11)
    key_first, key_second, key_spot = jax.random.split(base, 3)
    first_row = jax.random.randint(key_first, (HEADS,), 0, R1)
    second_row = jax.random.randint(key_second, (HEADS,), 0, R2)
    spot = jax.random.randint(key_spot, (), 0, HEADS)
    second_row = jnp.where(jnp.arange(HEADS) == spot, R2 - 1, second_row)
    return jnp.stack([first_row, second_row]).astype(jnp.int32)


def block_levels(own_key, dims, cuts, low, top_value):
    factor_of = 1.0
    for position, blocks in cuts:
        steps = jax.random.uniform(jax.random.fold_in(jax.random.fold_in(own_key, 6), position), (blocks,), jnp.float32, low / len(cuts), top_value / len(cuts))
        factor_of = factor_of * jnp.repeat(jnp.exp(steps), dims[position] // blocks).reshape((-1,) + (1,) * (len(dims) - 1 - position))
    return factor_of


def normal_values(key, shape, spread, reach, shards=(), held_as=jnp.bfloat16):
    values = spread * jax.random.normal(key, shape, jnp.float32)
    if shards:
        values = values * block_levels(key, shape, shards, -0.22, 0.18)
    return jnp.clip(values, -reach, reach).astype(held_as)


def setup_inputs(seed: int = 0) -> dict:
    arg_keys = jax.random.split(jax.random.key(seed), 6)
    return {
        "queries": draw_queries(jax.random.fold_in(arg_keys[5], 71), 0),
        "key_rows": draw_key_rows(jax.random.fold_in(arg_keys[5], 71), 0),
        "value_rows": normal_values(arg_keys[2], (TOKENS, WIDTH), 1.0, 6.0, ((0, 512),)),
        "rel_bias": normal_values(arg_keys[3], (BUCKETS, HEADS), 1.0, 4.0, ((1, 4),), jnp.float32),
        "offsets": draw_offsets(jax.random.fold_in(arg_keys[5], 71), 0),
    }


def bucket_edges():
    half_count = BUCKETS // 2
    thresholds = []
    for target in range(half_count + 1, BUCKETS):
        thresholds.append(int(math.ceil(half_count * (MAXDIST / half_count) ** ((target - half_count) / half_count))))
    return thresholds


def bucket_of(token_separation):
    half_count = BUCKETS // 2
    far_bucket = jnp.full(token_separation.shape, half_count, jnp.int32)
    for border in bucket_edges():
        far_bucket = far_bucket + (token_separation >= border).astype(jnp.int32)
    return jnp.where(token_separation < half_count, token_separation, far_bucket)


def bias_block(position_bias_lookup, ask_count, key_count, advance, stride):
    band_len = ask_count + key_count
    spots = jnp.arange(band_len, dtype=jnp.int32)
    token_separation = jnp.maximum((spots - (key_count - 1) + advance) * stride, 0)
    indicator_matrix = (bucket_of(token_separation)[:, None] == jnp.arange(BUCKETS, dtype=jnp.int32)[None, :]).astype(position_bias_lookup.dtype)
    column_vals = jnp.transpose(jnp.dot(indicator_matrix, position_bias_lookup, precision=lax.Precision.HIGHEST))
    lookup = jnp.arange(ask_count, dtype=jnp.int32)[:, None] - jnp.arange(key_count, dtype=jnp.int32)[None, :] + (key_count - 1)
    return jnp.take(column_vals, lookup, axis=1)


def start_state(ask_count, n_heads, head_dim):
    return (jnp.full((n_heads, ask_count), -1e30, jnp.float32), jnp.zeros((n_heads, ask_count), jnp.float32), jnp.zeros((ask_count, n_heads, head_dim), jnp.float32))


def attend(running, asks, key_part, value_part, advance, stride, position_bias_lookup, usable):
    ask_count = asks.shape[0]
    key_count = key_part.shape[0]
    scores = jnp.einsum("qhd,khd->hqk", asks.astype(jnp.float32), key_part.astype(jnp.float32)) * (asks.shape[2] ** -0.5)
    scores = scores + bias_block(position_bias_lookup, ask_count, key_count, advance, stride)
    allowed = (jnp.arange(ask_count, dtype=jnp.int32)[:, None] + advance >= jnp.arange(key_count, dtype=jnp.int32)[None, :]) & usable
    held = jnp.where(allowed[None], scores, -1e30)
    row_top, row_sum, row_acc = running
    fresh = jnp.maximum(row_top, jnp.max(held, axis=2))
    weights = jnp.where(allowed[None], jnp.exp(held - fresh[:, :, None]), 0.0)
    shrink = jnp.exp(row_top - fresh)
    row_sum = row_sum * shrink + jnp.sum(weights, axis=2)
    rounded = lax.optimization_barrier(weights.astype(jnp.bfloat16))
    blended = jnp.einsum("hqk,khd->qhd", rounded.astype(jnp.float32), value_part.astype(jnp.float32))
    row_acc = row_acc * jnp.transpose(shrink)[:, :, None] + blended
    return (fresh, row_sum, row_acc)


def finish(running):
    row_top, row_sum, row_acc = running
    result = (row_acc / jnp.transpose(row_sum)[:, :, None]).astype(jnp.bfloat16)
    return result, jnp.transpose(row_top + jnp.log(row_sum))


def select_rows(tokens, picks, stride):
    n_rows, n_heads, head_dim = tokens.shape
    grouped = tokens.reshape(n_rows // stride, stride, n_heads, head_dim)
    pick_index = jnp.broadcast_to(picks.astype(jnp.int32)[None, None, :, None], (n_rows // stride, 1, n_heads, head_dim))
    return jnp.take_along_axis(grouped, pick_index, axis=1).reshape(n_rows // stride, n_heads, head_dim)


def merge_block(first_out, leading_logsumexp, mid_out, mid_lse, far_out, far_lse, mid_pick, far_pick):
    long_rate = first_out.shape[1]
    spots = jnp.arange(long_rate, dtype=jnp.int32)[:, None]
    mid_cover = (spots % R1 == mid_pick.astype(jnp.int32)[None, :])[None]
    far_cover = (spots == far_pick.astype(jnp.int32)[None, :])[None]
    mid_lse_wide = jnp.repeat(mid_lse, R1, axis=1)
    mid_out_wide = jnp.repeat(mid_out, R1, axis=1)
    far_lse_wide = jnp.broadcast_to(far_lse[:, None, :], leading_logsumexp.shape)
    peak = jnp.maximum(leading_logsumexp, jnp.maximum(jnp.where(mid_cover, mid_lse_wide, leading_logsumexp), jnp.where(far_cover, far_lse_wide, leading_logsumexp)))
    first_weight = jnp.exp(leading_logsumexp - peak)
    mid_weight = jnp.where(mid_cover, jnp.exp(jnp.where(mid_cover, mid_lse_wide, peak) - peak), 0.0)
    far_weight = jnp.where(far_cover, jnp.exp(jnp.where(far_cover, far_lse_wide, peak) - peak), 0.0)
    blended = first_weight[..., None] * first_out.astype(jnp.float32) + mid_weight[..., None] * mid_out_wide.astype(jnp.float32) + far_weight[..., None] * far_out[:, None].astype(jnp.float32)
    return (blended / (first_weight + mid_weight + far_weight)[..., None]).astype(jnp.bfloat16)


def branch(asks, key_part, value_part, position_bias_lookup, picks, stride):
    chosen_q = select_rows(asks, picks, stride)
    chosen_k = select_rows(key_part, picks, stride)
    chosen_v = select_rows(value_part, picks, stride)
    n_segs = chosen_q.shape[0] // SPAN
    seg_shape = (n_segs, SPAN) + chosen_q.shape[1:]

    def single_segment_view(segment_parts):
        seg_q, seg_k, seg_v = segment_parts
        running = start_state(SPAN, seg_q.shape[1], seg_q.shape[2])
        return finish(attend(running, seg_q, seg_k, seg_v, 0, stride, position_bias_lookup, True))

    seg_outs, seg_lse = lax.map(single_segment_view, (chosen_q.reshape(seg_shape), chosen_k.reshape(seg_shape), chosen_v.reshape(seg_shape)))
    return seg_outs.reshape(chosen_q.shape), seg_lse.reshape(chosen_q.shape[:2])


def reference(queries, key_rows, value_rows, rel_bias, offsets):
    total_rows = queries.shape[0]
    asks = queries.reshape(total_rows, HEADS, DH)
    key_part = key_rows.reshape(total_rows, HEADS, DH)
    value_part = value_rows.reshape(total_rows, HEADS, DH)
    long_rate = total_rows // SPAN
    zero_pick = jnp.zeros((HEADS,), jnp.int32)
    first_out, leading_logsumexp = branch(asks, key_part, value_part, rel_bias, zero_pick, 1)
    mid_out, mid_lse = branch(asks, key_part, value_part, rel_bias, offsets[0], R1)
    far_out, far_lse = branch(asks, key_part, value_part, rel_bias, offsets[1], long_rate)

    def merge_one(block_parts):
        first_o, first_l, mid_o, mid_l, far_o, far_l = block_parts
        combined_block_result = merge_block(first_o[None], first_l[None], mid_o[None], mid_l[None], far_o[None], far_l[None], offsets[0], offsets[1])
        return combined_block_result[0]

    merged = lax.map(merge_one, (first_out.reshape(SPAN, long_rate, HEADS, DH), leading_logsumexp.reshape(SPAN, long_rate, HEADS), mid_out.reshape(SPAN, long_rate // R1, HEADS, DH), mid_lse.reshape(SPAN, long_rate // R1, HEADS), far_out, far_lse))
    return merged.reshape(total_rows, HEADS * DH)
```

```python
import math

import jax
import jax.numpy as jnp
from jax import lax
from jax.experimental import pallas as pl
from jax.experimental.pallas import tpu as pltpu
from jax.sharding import Mesh, PartitionSpec as P

DH = 128
BUCKETS = 32
MAXDIST = 128
R1 = 4
R2 = 64
SPAN = 256
PLANES = 16
GROUPS = 8
LANES = 4
PEERS = GROUPS * LANES
ROWS = 32
SEG = PEERS * ROWS
KEPT = SEG // R2
NEG = -1e30
SCALE = DH ** (-0.5)

VMEM = pl.BlockSpec(memory_space=pltpu.VMEM)
SMEM = pl.BlockSpec(memory_space=pltpu.SMEM)


def params():
    return pltpu.CompilerParams(vmem_limit_bytes=24 * 1024 * 1024)


def bucket_starts():
    half = BUCKETS // 2
    starts = list(range(half + 1))
    for target in range(half + 1, BUCKETS):
        starts.append(int(math.ceil(half * (MAXDIST / half) ** ((target - half) / half))))
    return starts


def pack_kernel(q_ref, k_ref, v_ref, out_ref):
    for g in range(GROUPS):
        for x in range(LANES):
            s, h = g * LANES + x, GROUPS * x + g
            cols = slice(h * DH, (h + 1) * DH)
            out_ref[s, 0:ROWS] = q_ref[:, cols]
            out_ref[s, ROWS : 2 * ROWS] = k_ref[:, cols]
            out_ref[s, 2 * ROWS : 3 * ROWS] = v_ref[:, cols]


def unpack_kernel(in_ref, out_ref):
    for g in range(GROUPS):
        for x in range(LANES):
            s, h = g * LANES + x, GROUPS * x + g
            out_ref[:, h * DH : (h + 1) * DH] = in_ref[s]


def bias_kernel(table_ref, where_ref, near_ref, mid_ref, far_ref):
    starts = bucket_starts()
    width = 2 * SPAN
    lane = lax.broadcasted_iota(jnp.int32, (8, width), 1)
    steps = jnp.where(lane == 0, 0, width - lane)

    def line(stride):
        distance = steps * stride
        value = jnp.full((8, width), table_ref[0, 0], jnp.float32)
        for n in range(1, BUCKETS):
            value = jnp.where(distance >= starts[n], table_ref[n, 0], value)
        return jnp.where((lane == 0) | (lane > SPAN), value, NEG)

    def spread(row, count):
        wide = jnp.broadcast_to(row[0:1], (count, width))
        return pltpu.roll(wide, 0, 1, stride=1, stride_axis=0)[:, :SPAN]

    near_ref[...] = spread(line(1), SPAN)
    mid_ref[...] = spread(line(R1), SPAN)
    far_ref[...] = spread(pltpu.roll(line(R2), where_ref[2] * KEPT, 1), KEPT)


def kept_tile(ref, part, pick):
    half = pick // ROWS
    within = pick % ROWS
    tile = (within // 16) * 16
    rows = ref[:, half, pl.ds(pl.multiple_of(part * ROWS + tile, 16), 16), :].astype(jnp.float32)
    spot = lax.broadcasted_iota(jnp.int32, (KEPT, 16, DH), 1)
    return jnp.sum(jnp.where(spot == within - tile, rows, 0.0), axis=1)


def kept_kernel(where_ref, qkv_ref, out_ref):
    pick = where_ref[1]
    keys = kept_tile(qkv_ref, 1, pick).astype(jnp.bfloat16)
    values = kept_tile(qkv_ref, 2, pick).astype(jnp.bfloat16)
    for z in range(PLANES):
        out_ref[z, 0:KEPT] = keys
        out_ref[z, KEPT : 2 * KEPT] = values


def branch(q, k, v, bias):
    scores = lax.dot_general(
        q, k, (((1,), (1,)), ((), ())), preferred_element_type=jnp.float32
    ) * SCALE + bias
    top = jnp.max(scores, axis=1, keepdims=True)
    weight = jnp.exp(scores - top)
    total = jnp.sum(weight, axis=1, keepdims=True)
    acc = jnp.dot(weight.astype(jnp.bfloat16), v, preferred_element_type=jnp.float32)
    shape = acc.shape
    return acc, jnp.broadcast_to(top, shape), jnp.broadcast_to(total, shape)


def merge(one, two):
    acc1, top1, total1 = one
    acc2, top2, total2 = two
    top = jnp.maximum(top1, top2)
    w1, w2 = jnp.exp(top1 - top), jnp.exp(top2 - top)
    return acc1 * w1 + acc2 * w2, top, total1 * w1 + total2 * w2


def local_kernel(
    where_ref, qkv_ref, near_ref, mid_ref, out_ref, far_ref, wide, acc_ref, top_ref, total_ref
):
    near_bias = near_ref[...]
    count = SPAN // ROWS
    for s in range(SEG // SPAN):
        blocks = slice(s * count, (s + 1) * count)
        rows = slice(s * SPAN, (s + 1) * SPAN)
        q = qkv_ref[blocks, 0:ROWS].reshape(SPAN, DH)
        k = qkv_ref[blocks, ROWS : 2 * ROWS].reshape(SPAN, DH)
        v = qkv_ref[blocks, 2 * ROWS : 3 * ROWS].reshape(SPAN, DH)
        wide[0, rows] = q.astype(jnp.float32)
        wide[1, rows] = k.astype(jnp.float32)
        wide[2, rows] = v.astype(jnp.float32)
        acc_ref[rows], top_ref[rows], total_ref[rows] = branch(q, k, v, near_bias)
    kept = pl.ds(where_ref[0], SPAN, stride=R1)
    q, k, v = (wide[n, kept, :].astype(jnp.bfloat16) for n in range(3))
    mid = branch(q, k, v, mid_ref[...])
    merged = merge((acc_ref[kept, :], top_ref[kept, :], total_ref[kept, :]), mid)
    acc_ref[kept, :], top_ref[kept, :], total_ref[kept, :] = merged
    out_ref[...] = (acc_ref[...] / total_ref[...]).astype(jnp.bfloat16).reshape(PEERS, ROWS, DH)
    far = pl.ds(where_ref[1], KEPT, stride=R2)
    far_ref[0] = acc_ref[far, :]
    far_ref[1] = top_ref[far, :]
    far_ref[2] = total_ref[far, :]
    far_ref[3] = wide[0, far, :]


def far_kernel(where_ref, kv_ref, bias_ref, far_ref, in_ref, out_ref):
    q = far_ref[3].astype(jnp.bfloat16)
    k = kv_ref[:, 0:KEPT].reshape(SPAN, DH)
    v = kv_ref[:, KEPT : 2 * KEPT].reshape(SPAN, DH)
    far = branch(q, k, v, bias_ref[...])
    acc, _, total = merge((far_ref[0], far_ref[1], far_ref[2]), far)
    row = (acc / total).astype(jnp.bfloat16).astype(jnp.float32)
    out_ref[...] = in_ref[...]
    pick = where_ref[1]
    half = pick // ROWS
    within = pick % ROWS
    tile = (within // 16) * 16
    spot = lax.broadcasted_iota(jnp.int32, (KEPT, 16, DH), 1)
    rows = pl.ds(pl.multiple_of(tile, 16), 16)
    old = in_ref[:, half, rows, :].astype(jnp.float32)
    new = jnp.where(spot == within - tile, jnp.broadcast_to(row[:, None], old.shape), old)
    out_ref[:, half, rows, :] = new.astype(jnp.bfloat16)


def on_device(queries, key_rows, value_rows, rel_bias, offsets):
    bf16, f32 = jnp.bfloat16, jnp.float32
    group = lax.axis_index("g")
    table = lax.dynamic_slice_in_dim(rel_bias, group, 1, axis=1)
    picks = lax.dynamic_slice_in_dim(offsets, group, 1, axis=1)[:, 0]
    where = jnp.concatenate([picks, lax.axis_index("z").astype(jnp.int32)[None]])
    packed = pl.pallas_call(
        pack_kernel,
        out_shape=jax.ShapeDtypeStruct((PEERS, 3 * ROWS, DH), bf16),
        in_specs=[VMEM] * 3,
        out_specs=VMEM,
        compiler_params=params(),
        name="pack",
    )(queries, key_rows, value_rows)
    near_bias, mid_bias, far_bias = pl.pallas_call(
        bias_kernel,
        out_shape=(
            jax.ShapeDtypeStruct((SPAN, SPAN), f32),
            jax.ShapeDtypeStruct((SPAN, SPAN), f32),
            jax.ShapeDtypeStruct((KEPT, SPAN), f32),
        ),
        in_specs=[SMEM, SMEM],
        out_specs=(VMEM, VMEM, VMEM),
        compiler_params=params(),
        name="bias",
    )(table, where)
    qkv = lax.all_to_all(packed, ("g", "x"), 0, 0, tiled=True)
    kept = pl.pallas_call(
        kept_kernel,
        out_shape=jax.ShapeDtypeStruct((PLANES, 2 * KEPT, DH), bf16),
        in_specs=[SMEM, VMEM],
        out_specs=VMEM,
        compiler_params=params(),
        name="kept",
    )(where, qkv.reshape(KEPT, 2, 3 * ROWS, DH))
    kept = lax.all_to_all(kept, "z", 0, 0, tiled=True)
    local, far_parts = pl.pallas_call(
        local_kernel,
        out_shape=(
            jax.ShapeDtypeStruct((PEERS, ROWS, DH), bf16),
            jax.ShapeDtypeStruct((4, KEPT, DH), f32),
        ),
        in_specs=[SMEM, VMEM, VMEM, VMEM],
        out_specs=(VMEM, VMEM),
        scratch_shapes=[
            pltpu.VMEM((3, SEG, DH), f32),
            pltpu.VMEM((SEG, DH), f32),
            pltpu.VMEM((SEG, DH), f32),
            pltpu.VMEM((SEG, DH), f32),
        ],
        compiler_params=params(),
        name="local",
    )(where, qkv, near_bias, mid_bias)
    merged = pl.pallas_call(
        far_kernel,
        out_shape=jax.ShapeDtypeStruct((KEPT, 2, ROWS, DH), bf16),
        in_specs=[SMEM, VMEM, VMEM, VMEM, VMEM],
        out_specs=VMEM,
        input_output_aliases={4: 0},
        compiler_params=params(),
        name="far",
    )(where, kept, far_bias, far_parts, local.reshape(KEPT, 2, ROWS, DH))
    back = lax.all_to_all(merged.reshape(PEERS, ROWS, DH), ("g", "x"), 0, 0, tiled=True)
    return pl.pallas_call(
        unpack_kernel,
        out_shape=jax.ShapeDtypeStruct((ROWS, PEERS * DH), bf16),
        in_specs=[VMEM],
        out_specs=VMEM,
        compiler_params=params(),
        name="unpack",
    )(back)


def solution(mesh):
    mesh = Mesh(mesh.devices.reshape(PLANES, GROUPS, LANES), ("z", "g", "x"))
    rows = P(("z", "g", "x"), None)
    return jax.shard_map(
        on_device,
        mesh=mesh,
        in_specs=(rows, rows, rows, P(None, "x"), P(None, "x")),
        out_specs=rows,
        check_vma=False,
    )
```

```python
import math

import jax
import jax.numpy as jnp
from jax import lax
from jax.experimental import pallas as pl
from jax.experimental.pallas import tpu as pltpu
from jax.sharding import Mesh, PartitionSpec as P

DH = 128
BUCKETS = 32
MAXDIST = 128
R1 = 4
R2 = 64
SPAN = 256
PLANES = 16
GROUPS = 8
LANES = 4
PEERS = GROUPS * LANES
ROWS = 32
SEG = PEERS * ROWS
KEPT = SEG // R2
NEG = -1e30
SCALE = DH ** (-0.5)

VMEM = pl.BlockSpec(memory_space=pltpu.VMEM)
SMEM = pl.BlockSpec(memory_space=pltpu.SMEM)
HBM = pl.BlockSpec(memory_space=pltpu.HBM)


def params():
    return pltpu.CompilerParams(vmem_limit_bytes=24 * 1024 * 1024)


def bucket_starts():
    half = BUCKETS // 2
    starts = list(range(half + 1))
    for target in range(half + 1, BUCKETS):
        starts.append(int(math.ceil(half * (MAXDIST / half) ** ((target - half) / half))))
    return starts


def pack_kernel(q_ref, k_ref, v_ref, offsets_ref, out_ref, picks_ref, sems):
    copies = [pltpu.make_async_copy(offsets_ref, picks_ref, sems.at[3])]
    for n, ref in enumerate((q_ref, k_ref, v_ref)):
        for g in range(GROUPS):
            for x in range(LANES):
                s, h = g * LANES + x, GROUPS * x + g
                copies.append(
                    pltpu.make_async_copy(
                        ref.at[:, h * DH : (h + 1) * DH],
                        out_ref.at[s, n * ROWS : (n + 1) * ROWS],
                        sems.at[n],
                    )
                )
    for copy in copies:
        copy.start()
    for copy in copies:
        copy.wait()


def offset_of(ref, row):
    values = ref[...]
    at_row = lax.broadcasted_iota(jnp.int32, values.shape, 0) == row
    at_head = lax.broadcasted_iota(jnp.int32, values.shape, 1) == lax.axis_index("g")
    return jnp.sum(jnp.where(at_row & at_head, values, 0))


def unpack_kernel(in_ref, out_ref):
    for g in range(GROUPS):
        for x in range(LANES):
            s, h = g * LANES + x, GROUPS * x + g
            out_ref[:, h * DH : (h + 1) * DH] = in_ref[s]


def bias_kernel(table_ref, near_ref, mid_ref, far_ref):
    starts = bucket_starts()
    head = lax.axis_index("g")
    width = 2 * SPAN
    lane = lax.broadcasted_iota(jnp.int32, (8, width), 1)
    steps = jnp.where(lane == 0, 0, width - lane)

    def line(stride):
        distance = steps * stride
        value = jnp.full((8, width), table_ref[0, head], jnp.float32)
        for n in range(1, BUCKETS):
            value = jnp.where(distance >= starts[n], table_ref[n, head], value)
        return jnp.where((lane == 0) | (lane > SPAN), value, NEG)

    def spread(row, count):
        wide = jnp.broadcast_to(row[0:1], (count, width))
        return pltpu.roll(wide, 0, 1, stride=1, stride_axis=0)[:, :SPAN]

    near_ref[...] = spread(line(1), SPAN)
    mid_ref[...] = spread(line(R1), SPAN)
    far_ref[...] = spread(pltpu.roll(line(R2), lax.axis_index("z") * KEPT, 1), KEPT)


def kept_tile(ref, part, pick):
    half = pick // ROWS
    within = pick % ROWS
    tile = (within // 16) * 16
    rows = ref[:, half, pl.ds(pl.multiple_of(part * ROWS + tile, 16), 16), :].astype(jnp.float32)
    spot = lax.broadcasted_iota(jnp.int32, (KEPT, 16, DH), 1)
    return jnp.sum(jnp.where(spot == within - tile, rows, 0.0), axis=1)


def kept_kernel(offsets_ref, qkv_ref, out_ref):
    pick = offset_of(offsets_ref, 1)
    keys = kept_tile(qkv_ref, 1, pick).astype(jnp.bfloat16)
    values = kept_tile(qkv_ref, 2, pick).astype(jnp.bfloat16)
    for z in range(PLANES):
        out_ref[z, 0:KEPT] = keys
        out_ref[z, KEPT : 2 * KEPT] = values


def branch(q, k, v, bias):
    scores = lax.dot_general(
        q, k, (((1,), (1,)), ((), ())), preferred_element_type=jnp.float32
    ) * SCALE + bias
    top = jnp.max(scores, axis=1, keepdims=True)
    weight = jnp.exp(scores - top)
    total = jnp.sum(weight, axis=1, keepdims=True)
    acc = jnp.dot(weight.astype(jnp.bfloat16), v, preferred_element_type=jnp.float32)
    shape = acc.shape
    return acc, jnp.broadcast_to(top, shape), jnp.broadcast_to(total, shape)


def merge(one, two):
    acc1, top1, total1 = one
    acc2, top2, total2 = two
    top = jnp.maximum(top1, top2)
    w1, w2 = jnp.exp(top1 - top), jnp.exp(top2 - top)
    return acc1 * w1 + acc2 * w2, top, total1 * w1 + total2 * w2


def local_kernel(
    offsets_ref, qkv_ref, near_ref, mid_ref, out_ref, far_ref, wide, acc_ref, top_ref, total_ref
):
    near_bias = near_ref[...]
    count = SPAN // ROWS
    for s in range(SEG // SPAN):
        blocks = slice(s * count, (s + 1) * count)
        rows = slice(s * SPAN, (s + 1) * SPAN)
        q = qkv_ref[blocks, 0:ROWS].reshape(SPAN, DH)
        k = qkv_ref[blocks, ROWS : 2 * ROWS].reshape(SPAN, DH)
        v = qkv_ref[blocks, 2 * ROWS : 3 * ROWS].reshape(SPAN, DH)
        wide[0, rows] = q.astype(jnp.float32)
        wide[1, rows] = k.astype(jnp.float32)
        wide[2, rows] = v.astype(jnp.float32)
        acc_ref[rows], top_ref[rows], total_ref[rows] = branch(q, k, v, near_bias)
    kept = pl.ds(offset_of(offsets_ref, 0), SPAN, stride=R1)
    q, k, v = (wide[n, kept, :].astype(jnp.bfloat16) for n in range(3))
    mid = branch(q, k, v, mid_ref[...])
    merged = merge((acc_ref[kept, :], top_ref[kept, :], total_ref[kept, :]), mid)
    acc_ref[kept, :], top_ref[kept, :], total_ref[kept, :] = merged
    out_ref[...] = (acc_ref[...] / total_ref[...]).astype(jnp.bfloat16).reshape(PEERS, ROWS, DH)
    far = pl.ds(offset_of(offsets_ref, 1), KEPT, stride=R2)
    far_ref[0] = acc_ref[far, :]
    far_ref[1] = top_ref[far, :]
    far_ref[2] = total_ref[far, :]
    far_ref[3] = wide[0, far, :]


def far_kernel(offsets_ref, kv_ref, bias_ref, far_ref, in_ref, out_ref):
    q = far_ref[3].astype(jnp.bfloat16)
    k = kv_ref[:, 0:KEPT].reshape(SPAN, DH)
    v = kv_ref[:, KEPT : 2 * KEPT].reshape(SPAN, DH)
    far = branch(q, k, v, bias_ref[...])
    acc, _, total = merge((far_ref[0], far_ref[1], far_ref[2]), far)
    row = (acc / total).astype(jnp.bfloat16).astype(jnp.float32)
    out_ref[...] = in_ref[...]
    pick = offset_of(offsets_ref, 1)
    half = pick // ROWS
    within = pick % ROWS
    tile = (within // 16) * 16
    spot = lax.broadcasted_iota(jnp.int32, (KEPT, 16, DH), 1)
    rows = pl.ds(pl.multiple_of(tile, 16), 16)
    old = in_ref[:, half, rows, :].astype(jnp.float32)
    new = jnp.where(spot == within - tile, jnp.broadcast_to(row[:, None], old.shape), old)
    out_ref[:, half, rows, :] = new.astype(jnp.bfloat16)


def on_device(queries, key_rows, value_rows, rel_bias, offsets):
    bf16, f32 = jnp.bfloat16, jnp.float32
    given = (queries, key_rows, value_rows, offsets)
    packed, picks = pl.pallas_call(
        pack_kernel,
        out_shape=(
            jax.ShapeDtypeStruct((PEERS, 3 * ROWS, DH), bf16),
            jax.ShapeDtypeStruct(offsets.shape, offsets.dtype),
        ),
        in_specs=[HBM] * 4,
        out_specs=(VMEM, VMEM),
        scratch_shapes=[pltpu.SemaphoreType.DMA((4,))],
        compiler_params=params(),
        name="pack",
    )(*(pltpu.with_memory_space_constraint(t, pltpu.HBM) for t in given))
    qkv = lax.all_to_all(packed, ("g", "x"), 0, 0, tiled=True)
    kept = pl.pallas_call(
        kept_kernel,
        out_shape=jax.ShapeDtypeStruct((PLANES, 2 * KEPT, DH), bf16),
        in_specs=[VMEM, VMEM],
        out_specs=VMEM,
        compiler_params=params(),
        name="kept",
    )(picks, qkv.reshape(KEPT, 2, 3 * ROWS, DH))
    kept = lax.all_to_all(kept, "z", 0, 0, tiled=True)
    near_bias, mid_bias, far_bias = pl.pallas_call(
        bias_kernel,
        out_shape=(
            jax.ShapeDtypeStruct((SPAN, SPAN), f32),
            jax.ShapeDtypeStruct((SPAN, SPAN), f32),
            jax.ShapeDtypeStruct((KEPT, SPAN), f32),
        ),
        in_specs=[SMEM],
        out_specs=(VMEM, VMEM, VMEM),
        compiler_params=params(),
        name="bias",
    )(rel_bias)
    local, far_parts = pl.pallas_call(
        local_kernel,
        out_shape=(
            jax.ShapeDtypeStruct((PEERS, ROWS, DH), bf16),
            jax.ShapeDtypeStruct((4, KEPT, DH), f32),
        ),
        in_specs=[VMEM] * 4,
        out_specs=(VMEM, VMEM),
        scratch_shapes=[
            pltpu.VMEM((3, SEG, DH), f32),
            pltpu.VMEM((SEG, DH), f32),
            pltpu.VMEM((SEG, DH), f32),
            pltpu.VMEM((SEG, DH), f32),
        ],
        compiler_params=params(),
        name="local",
    )(picks, qkv, near_bias, mid_bias)
    merged = pl.pallas_call(
        far_kernel,
        out_shape=jax.ShapeDtypeStruct((KEPT, 2, ROWS, DH), bf16),
        in_specs=[VMEM] * 5,
        out_specs=VMEM,
        input_output_aliases={4: 0},
        compiler_params=params(),
        name="far",
    )(picks, kept, far_bias, far_parts, local.reshape(KEPT, 2, ROWS, DH))
    back = lax.all_to_all(merged.reshape(PEERS, ROWS, DH), ("g", "x"), 0, 0, tiled=True)
    return pl.pallas_call(
        unpack_kernel,
        out_shape=jax.ShapeDtypeStruct((ROWS, PEERS * DH), bf16),
        in_specs=[VMEM],
        out_specs=VMEM,
        compiler_params=params(),
        name="unpack",
    )(back)


def solution(mesh):
    mesh = Mesh(mesh.devices.reshape(PLANES, GROUPS, LANES), ("z", "g", "x"))
    rows = P(("z", "g", "x"), None)
    return jax.shard_map(
        on_device,
        mesh=mesh,
        in_specs=(rows, rows, rows, P(None, "x"), P(None, "x")),
        out_specs=rows,
        check_vma=False,
    )
```

```python
import math

import jax
import jax.numpy as jnp
from jax import lax
from jax.experimental import pallas as pl
from jax.experimental.pallas import tpu as pltpu
from jax.sharding import Mesh, PartitionSpec as P

DH = 128
BUCKETS = 32
MAXDIST = 128
R1 = 4
R2 = 64
SPAN = 256
PLANES = 16
GROUPS = 8
LANES = 4
PEERS = GROUPS * LANES
ROWS = 32
SEG = PEERS * ROWS
KEPT = SEG // R2
RING = [8, 0, 1, 15, 2, 14, 3, 13, 4, 12, 5, 11, 6, 10, 7, 9]
ORDER_IN = [(2 * y + c) * LANES + x for c in (0, 1) for y in (3, 2, 1, 0) for x in (3, 2, 1, 0)]
ORDER_OUT = [(2 * y + c) * LANES + x for c in (0, 1) for y in (0, 1, 2, 3) for x in (0, 1, 2, 3)]
PAIRS_IN = [n // 2 for n in ORDER_IN[::2]]
PAIRS_OUT = [n // 2 for n in ORDER_OUT[::2]]
PLACE = {n: p for p, n in enumerate(ORDER_IN)}
NEG = -1e30
SCALE = DH ** (-0.5)

VMEM = pl.BlockSpec(memory_space=pltpu.VMEM)
SMEM = pl.BlockSpec(memory_space=pltpu.SMEM)
HBM = pl.BlockSpec(memory_space=pltpu.HBM)


def params():
    return pltpu.CompilerParams(vmem_limit_bytes=24 * 1024 * 1024)


def bucket_starts():
    half = BUCKETS // 2
    starts = list(range(half + 1))
    for target in range(half + 1, BUCKETS):
        starts.append(int(math.ceil(half * (MAXDIST / half) ** ((target - half) / half))))
    return starts


def pack_kernel(q_ref, k_ref, v_ref, offsets_ref, out_ref, picks_ref, sems):
    copies = [pltpu.make_async_copy(offsets_ref, picks_ref, sems.at[3])]
    for n, ref in enumerate((q_ref, k_ref, v_ref)):
        for g in range(GROUPS):
            for x in range(LANES):
                p, h = PLACE[g * LANES + x], GROUPS * x + g
                copies.append(
                    pltpu.make_async_copy(
                        ref.at[:, h * DH : (h + 1) * DH],
                        out_ref.at[p, n * ROWS : (n + 1) * ROWS],
                        sems.at[n],
                    )
                )
    for copy in copies:
        copy.start()
    for copy in copies:
        copy.wait()


def offset_of(ref, row):
    values = ref[...]
    at_row = lax.broadcasted_iota(jnp.int32, values.shape, 0) == row
    at_head = lax.broadcasted_iota(jnp.int32, values.shape, 1) == lax.axis_index("g")
    return jnp.sum(jnp.where(at_row & at_head, values, 0))


def unpack_kernel(in_ref, out_ref):
    for p, n in enumerate(ORDER_OUT):
        h = GROUPS * (n % LANES) + n // LANES
        out_ref[:, h * DH : (h + 1) * DH] = in_ref[p]


def bias_kernel(table_ref, near_ref, mid_ref, far_ref):
    starts = bucket_starts()
    head = lax.axis_index("g")
    width = 2 * SPAN
    lane = lax.broadcasted_iota(jnp.int32, (8, width), 1)
    steps = jnp.where(lane == 0, 0, width - lane)

    def value_at(distance):
        value = jnp.full(distance.shape, table_ref[0, head], jnp.float32)
        for n in range(1, BUCKETS):
            value = jnp.where(distance >= starts[n], table_ref[n, head], value)
        return value

    def line(stride):
        return jnp.where((lane == 0) | (lane > SPAN), value_at(steps * stride), NEG)

    def spread(row, count):
        wide = jnp.broadcast_to(row[0:1], (count, width))
        return pltpu.roll(wide, 0, 1, stride=1, stride_axis=0)[:, :SPAN]

    near_ref[...] = spread(line(1), SPAN)
    mid_ref[...] = spread(line(R1), SPAN)
    row = lax.broadcasted_iota(jnp.int32, (KEPT, SPAN), 0)
    column = lax.broadcasted_iota(jnp.int32, (KEPT, SPAN), 1)
    plane = jnp.zeros((KEPT, SPAN), jnp.int32)
    for n in range(PLANES):
        plane = jnp.where(column // KEPT == n, RING[n], plane)
    query, key = jnp.zeros((KEPT, SPAN), jnp.int32), jnp.zeros((KEPT, SPAN), jnp.int32)
    for n in range(KEPT):
        query = jnp.where(row == n, PAIRS_OUT[n], query)
        key = jnp.where(column % KEPT == n, PAIRS_IN[n], key)
    apart = (lax.axis_index("z") - plane) * KEPT + query - key
    far_ref[...] = jnp.where(apart >= 0, value_at(apart * R2), NEG)


def kept_tile(ref, part, pick):
    half = pick // ROWS
    within = pick % ROWS
    tile = (within // 16) * 16
    rows = ref[:, 1 - half, pl.ds(pl.multiple_of(part * ROWS + tile, 16), 16), :]
    spot = lax.broadcasted_iota(jnp.int32, (KEPT, 16, DH), 1)
    return jnp.sum(jnp.where(spot == within - tile, rows.astype(jnp.float32), 0.0), axis=1)


def kept_kernel(offsets_ref, qkv_ref, out_ref):
    pick = offset_of(offsets_ref, 1)
    keys = kept_tile(qkv_ref, 1, pick).astype(jnp.bfloat16)
    values = kept_tile(qkv_ref, 2, pick).astype(jnp.bfloat16)
    for z in range(PLANES):
        out_ref[z, 0:KEPT] = keys
        out_ref[z, KEPT : 2 * KEPT] = values


def branch(q, k, v, bias):
    scores = lax.dot_general(
        q, k, (((1,), (1,)), ((), ())), preferred_element_type=jnp.float32
    ) * SCALE + bias
    top = jnp.max(scores, axis=1, keepdims=True)
    weight = jnp.exp(scores - top)
    total = jnp.sum(weight, axis=1, keepdims=True)
    acc = jnp.dot(weight.astype(jnp.bfloat16), v, preferred_element_type=jnp.float32)
    shape = acc.shape
    return acc, jnp.broadcast_to(top, shape), jnp.broadcast_to(total, shape)


def merge(one, two):
    acc1, top1, total1 = one
    acc2, top2, total2 = two
    top = jnp.maximum(top1, top2)
    w1, w2 = jnp.exp(top1 - top), jnp.exp(top2 - top)
    return acc1 * w1 + acc2 * w2, top, total1 * w1 + total2 * w2


def local_kernel(
    offsets_ref, qkv_ref, near_ref, mid_ref, out_ref, far_ref, wide, acc_ref, top_ref, total_ref
):
    near_bias = near_ref[...]
    count = SPAN // ROWS
    for s in range(SEG // SPAN):
        blocks = [PLACE[n] for n in range(s * count, (s + 1) * count)]
        rows = slice(s * SPAN, (s + 1) * SPAN)
        q, k, v = (
            jnp.concatenate([qkv_ref[p, n * ROWS : (n + 1) * ROWS] for p in blocks], axis=0)
            for n in range(3)
        )
        wide[0, rows] = q.astype(jnp.float32)
        wide[1, rows] = k.astype(jnp.float32)
        wide[2, rows] = v.astype(jnp.float32)
        acc_ref[rows], top_ref[rows], total_ref[rows] = branch(q, k, v, near_bias)
    kept = pl.ds(offset_of(offsets_ref, 0), SPAN, stride=R1)
    q, k, v = (wide[n, kept, :].astype(jnp.bfloat16) for n in range(3))
    mid = branch(q, k, v, mid_ref[...])
    merged = merge((acc_ref[kept, :], top_ref[kept, :], total_ref[kept, :]), mid)
    acc_ref[kept, :], top_ref[kept, :], total_ref[kept, :] = merged
    for p, n in enumerate(ORDER_OUT):
        rows = slice(n * ROWS, (n + 1) * ROWS)
        out_ref[p] = (acc_ref[rows] / total_ref[rows]).astype(jnp.bfloat16)
    far = pl.ds(offset_of(offsets_ref, 1), KEPT, stride=R2)
    parts = acc_ref[far, :], top_ref[far, :], total_ref[far, :], wide[0, far, :]
    for n, part in enumerate(parts):
        for m, pair in enumerate(PAIRS_OUT):
            far_ref[n, m : m + 1] = part[pair : pair + 1]


def far_kernel(offsets_ref, kv_ref, bias_ref, far_ref, in_ref, out_ref):
    q = far_ref[3].astype(jnp.bfloat16)
    k = kv_ref[:, 0:KEPT].reshape(SPAN, DH)
    v = kv_ref[:, KEPT : 2 * KEPT].reshape(SPAN, DH)
    far = branch(q, k, v, bias_ref[...])
    acc, _, total = merge((far_ref[0], far_ref[1], far_ref[2]), far)
    row = (acc / total).astype(jnp.bfloat16).astype(jnp.float32)
    out_ref[...] = in_ref[...]
    pick = offset_of(offsets_ref, 1)
    half = pick // ROWS
    within = pick % ROWS
    tile = (within // 16) * 16
    spot = lax.broadcasted_iota(jnp.int32, (KEPT, 16, DH), 1)
    rows = pl.ds(pl.multiple_of(tile, 16), 16)
    old = in_ref[:, half, rows, :].astype(jnp.float32)
    new = jnp.where(spot == within - tile, jnp.broadcast_to(row[:, None], old.shape), old)
    out_ref[:, half, rows, :] = new.astype(jnp.bfloat16)


def on_device(queries, key_rows, value_rows, rel_bias, offsets):
    bf16, f32 = jnp.bfloat16, jnp.float32
    given = (queries, key_rows, value_rows, offsets)
    packed, picks = pl.pallas_call(
        pack_kernel,
        out_shape=(
            jax.ShapeDtypeStruct((PEERS, 3 * ROWS, DH), bf16),
            jax.ShapeDtypeStruct(offsets.shape, offsets.dtype),
        ),
        in_specs=[HBM] * 4,
        out_specs=(VMEM, VMEM),
        scratch_shapes=[pltpu.SemaphoreType.DMA((4,))],
        compiler_params=params(),
        name="pack",
    )(*(pltpu.with_memory_space_constraint(t, pltpu.HBM) for t in given))
    qkv = lax.all_to_all(packed, ("g", "x"), 0, 0, axis_index_groups=[ORDER_IN], tiled=True)
    kept = pl.pallas_call(
        kept_kernel,
        out_shape=jax.ShapeDtypeStruct((PLANES, 2 * KEPT, DH), bf16),
        in_specs=[VMEM, VMEM],
        out_specs=VMEM,
        compiler_params=params(),
        name="kept",
    )(picks, qkv.reshape(KEPT, 2, 3 * ROWS, DH))
    kept = lax.all_to_all(kept, "z", 0, 0, axis_index_groups=[RING], tiled=True)
    near_bias, mid_bias, far_bias = pl.pallas_call(
        bias_kernel,
        out_shape=(
            jax.ShapeDtypeStruct((SPAN, SPAN), f32),
            jax.ShapeDtypeStruct((SPAN, SPAN), f32),
            jax.ShapeDtypeStruct((KEPT, SPAN), f32),
        ),
        in_specs=[SMEM],
        out_specs=(VMEM, VMEM, VMEM),
        compiler_params=params(),
        name="bias",
    )(rel_bias)
    local, far_parts = pl.pallas_call(
        local_kernel,
        out_shape=(
            jax.ShapeDtypeStruct((PEERS, ROWS, DH), bf16),
            jax.ShapeDtypeStruct((4, KEPT, DH), f32),
        ),
        in_specs=[VMEM] * 4,
        out_specs=(VMEM, VMEM),
        scratch_shapes=[
            pltpu.VMEM((3, SEG, DH), f32),
            pltpu.VMEM((SEG, DH), f32),
            pltpu.VMEM((SEG, DH), f32),
            pltpu.VMEM((SEG, DH), f32),
        ],
        compiler_params=params(),
        name="local",
    )(picks, qkv, near_bias, mid_bias)
    merged = pl.pallas_call(
        far_kernel,
        out_shape=jax.ShapeDtypeStruct((KEPT, 2, ROWS, DH), bf16),
        in_specs=[VMEM] * 5,
        out_specs=VMEM,
        input_output_aliases={4: 0},
        compiler_params=params(),
        name="far",
    )(picks, kept, far_bias, far_parts, local.reshape(KEPT, 2, ROWS, DH))
    back = lax.all_to_all(
        merged.reshape(PEERS, ROWS, DH),
        ("g", "x"),
        0,
        0,
        axis_index_groups=[ORDER_OUT],
        tiled=True,
    )
    return pl.pallas_call(
        unpack_kernel,
        out_shape=jax.ShapeDtypeStruct((ROWS, PEERS * DH), bf16),
        in_specs=[VMEM],
        out_specs=VMEM,
        compiler_params=params(),
        name="unpack",
    )(back)


def solution(mesh):
    mesh = Mesh(mesh.devices.reshape(PLANES, GROUPS, LANES), ("z", "g", "x"))
    rows = P(("z", "g", "x"), None)
    return jax.shard_map(
        on_device,
        mesh=mesh,
        in_specs=(rows, rows, rows, P(None, "x"), P(None, "x")),
        out_specs=rows,
        check_vma=False,
    )
```

```python
import math

import jax
import jax.numpy as jnp
from jax import lax
from jax.experimental import pallas as pl
from jax.experimental.pallas import tpu as pltpu
from jax.sharding import Mesh, PartitionSpec as P

DH = 128
BUCKETS = 32
MAXDIST = 128
R1 = 4
R2 = 64
SPAN = 256
PLANES = 16
GROUPS = 8
LANES = 4
PEERS = GROUPS * LANES
ROWS = 32
SEG = PEERS * ROWS
KEPT = SEG // R2
HALF = PLANES // 2
LOW = [5, 0, 1, 2, 3, 4, 6, 7]
HIGH = [11, 8, 9, 10, 12, 13, 14, 15]
ORDER_IN = [(2 * y + c) * LANES + x for c in (0, 1) for y in (3, 2, 1, 0) for x in (3, 2, 1, 0)]
ORDER_OUT = [(2 * y + c) * LANES + x for c in (0, 1) for y in (0, 1, 2, 3) for x in (0, 1, 2, 3)]
PAIRS_IN = [n // 2 for n in ORDER_IN[::2]]
PAIRS_OUT = [n // 2 for n in ORDER_OUT[::2]]
PLACE = {n: p for p, n in enumerate(ORDER_IN)}
NEG = -1e30
SCALE = DH ** (-0.5)

VMEM = pl.BlockSpec(memory_space=pltpu.VMEM)
SMEM = pl.BlockSpec(memory_space=pltpu.SMEM)
HBM = pl.BlockSpec(memory_space=pltpu.HBM)


def params():
    return pltpu.CompilerParams(vmem_limit_bytes=24 * 1024 * 1024)


def bucket_starts():
    half = BUCKETS // 2
    starts = list(range(half + 1))
    for target in range(half + 1, BUCKETS):
        starts.append(int(math.ceil(half * (MAXDIST / half) ** ((target - half) / half))))
    return starts


def pack_kernel(q_ref, k_ref, v_ref, offsets_ref, out_ref, picks_ref, sems):
    copies = [pltpu.make_async_copy(offsets_ref, picks_ref, sems.at[3])]
    for n, ref in enumerate((q_ref, k_ref, v_ref)):
        for g in range(GROUPS):
            for x in range(LANES):
                p, h = PLACE[g * LANES + x], GROUPS * x + g
                copies.append(
                    pltpu.make_async_copy(
                        ref.at[:, h * DH : (h + 1) * DH],
                        out_ref.at[p, n * ROWS : (n + 1) * ROWS],
                        sems.at[n],
                    )
                )
    for copy in copies:
        copy.start()
    for copy in copies:
        copy.wait()


def offset_of(ref, row):
    values = ref[...]
    at_row = lax.broadcasted_iota(jnp.int32, values.shape, 0) == row
    at_head = lax.broadcasted_iota(jnp.int32, values.shape, 1) == lax.axis_index("g")
    return jnp.sum(jnp.where(at_row & at_head, values, 0))


def unpack_kernel(in_ref, out_ref):
    for p, n in enumerate(ORDER_OUT):
        h = GROUPS * (n % LANES) + n // LANES
        out_ref[:, h * DH : (h + 1) * DH] = in_ref[p]


def bias_kernel(table_ref, near_ref, mid_ref, far_ref):
    starts = bucket_starts()
    head = lax.axis_index("g")
    width = 2 * SPAN
    lane = lax.broadcasted_iota(jnp.int32, (8, width), 1)
    steps = jnp.where(lane == 0, 0, width - lane)

    def value_at(distance):
        value = jnp.full(distance.shape, table_ref[0, head], jnp.float32)
        for n in range(1, BUCKETS):
            value = jnp.where(distance >= starts[n], table_ref[n, head], value)
        return value

    def line(stride):
        return jnp.where((lane == 0) | (lane > SPAN), value_at(steps * stride), NEG)

    def spread(row, count):
        wide = jnp.broadcast_to(row[0:1], (count, width))
        return pltpu.roll(wide, 0, 1, stride=1, stride_axis=0)[:, :SPAN]

    near_ref[...] = spread(line(1), SPAN)
    mid_ref[...] = spread(line(R1), SPAN)
    row = lax.broadcasted_iota(jnp.int32, (KEPT, SPAN), 0)
    column = lax.broadcasted_iota(jnp.int32, (KEPT, SPAN), 1)
    here = lax.axis_index("z")
    plane = jnp.full((KEPT, SPAN), PLANES, jnp.int32)
    for n in range(HALF):
        own = jnp.where(here < HALF, LOW[n], HIGH[n])
        other = jnp.where(here < HALF, PLANES, LOW[n])
        plane = jnp.where(column // KEPT == n, own, plane)
        plane = jnp.where(column // KEPT == n + HALF, other, plane)
    query, key = jnp.zeros((KEPT, SPAN), jnp.int32), jnp.zeros((KEPT, SPAN), jnp.int32)
    for n in range(KEPT):
        query = jnp.where(row == n, PAIRS_OUT[n], query)
        key = jnp.where(column % KEPT == n, PAIRS_IN[n], key)
    apart = (here - plane) * KEPT + query - key
    far_ref[...] = jnp.where(apart >= 0, value_at(apart * R2), NEG)


def kept_tile(ref, part, pick):
    half = pick // ROWS
    within = pick % ROWS
    tile = (within // 16) * 16
    rows = ref[:, 1 - half, pl.ds(pl.multiple_of(part * ROWS + tile, 16), 16), :]
    spot = lax.broadcasted_iota(jnp.int32, (KEPT, 16, DH), 1)
    return jnp.sum(jnp.where(spot == within - tile, rows.astype(jnp.float32), 0.0), axis=1)


def kept_kernel(offsets_ref, qkv_ref, out_ref):
    pick = offset_of(offsets_ref, 1)
    keys = kept_tile(qkv_ref, 1, pick).astype(jnp.bfloat16)
    values = kept_tile(qkv_ref, 2, pick).astype(jnp.bfloat16)
    for z in range(HALF):
        out_ref[z, 0:KEPT] = keys
        out_ref[z, KEPT : 2 * KEPT] = values


def branch(q, k, v, bias):
    scores = lax.dot_general(
        q, k, (((1,), (1,)), ((), ())), preferred_element_type=jnp.float32
    ) * SCALE + bias
    top = jnp.max(scores, axis=1, keepdims=True)
    weight = jnp.exp(scores - top)
    total = jnp.sum(weight, axis=1, keepdims=True)
    acc = jnp.dot(weight.astype(jnp.bfloat16), v, preferred_element_type=jnp.float32)
    shape = acc.shape
    return acc, jnp.broadcast_to(top, shape), jnp.broadcast_to(total, shape)


def merge(one, two):
    acc1, top1, total1 = one
    acc2, top2, total2 = two
    top = jnp.maximum(top1, top2)
    w1, w2 = jnp.exp(top1 - top), jnp.exp(top2 - top)
    return acc1 * w1 + acc2 * w2, top, total1 * w1 + total2 * w2


def local_kernel(
    offsets_ref, qkv_ref, near_ref, mid_ref, out_ref, far_ref, wide, acc_ref, top_ref, total_ref
):
    near_bias = near_ref[...]
    count = SPAN // ROWS
    for s in range(SEG // SPAN):
        blocks = [PLACE[n] for n in range(s * count, (s + 1) * count)]
        rows = slice(s * SPAN, (s + 1) * SPAN)
        q, k, v = (
            jnp.concatenate([qkv_ref[p, n * ROWS : (n + 1) * ROWS] for p in blocks], axis=0)
            for n in range(3)
        )
        wide[0, rows] = q.astype(jnp.float32)
        wide[1, rows] = k.astype(jnp.float32)
        wide[2, rows] = v.astype(jnp.float32)
        acc_ref[rows], top_ref[rows], total_ref[rows] = branch(q, k, v, near_bias)
    kept = pl.ds(offset_of(offsets_ref, 0), SPAN, stride=R1)
    q, k, v = (wide[n, kept, :].astype(jnp.bfloat16) for n in range(3))
    mid = branch(q, k, v, mid_ref[...])
    merged = merge((acc_ref[kept, :], top_ref[kept, :], total_ref[kept, :]), mid)
    acc_ref[kept, :], top_ref[kept, :], total_ref[kept, :] = merged
    for p, n in enumerate(ORDER_OUT):
        rows = slice(n * ROWS, (n + 1) * ROWS)
        out_ref[p] = (acc_ref[rows] / total_ref[rows]).astype(jnp.bfloat16)
    far = pl.ds(offset_of(offsets_ref, 1), KEPT, stride=R2)
    parts = acc_ref[far, :], top_ref[far, :], total_ref[far, :], wide[0, far, :]
    for n, part in enumerate(parts):
        for m, pair in enumerate(PAIRS_OUT):
            far_ref[n, m : m + 1] = part[pair : pair + 1]


def far_kernel(offsets_ref, bias_ref, far_ref, *refs):
    *kv_refs, in_ref, out_ref = refs
    q = far_ref[3].astype(jnp.bfloat16)
    kv = jnp.concatenate([ref[...] for ref in kv_refs], axis=0)
    count = kv.shape[0] * KEPT
    k = kv[:, 0:KEPT].reshape(count, DH)
    v = kv[:, KEPT : 2 * KEPT].reshape(count, DH)
    far = branch(q, k, v, bias_ref[:, 0:count])
    acc, _, total = merge((far_ref[0], far_ref[1], far_ref[2]), far)
    row = (acc / total).astype(jnp.bfloat16).astype(jnp.float32)
    out_ref[...] = in_ref[...]
    pick = offset_of(offsets_ref, 1)
    half = pick // ROWS
    within = pick % ROWS
    tile = (within // 16) * 16
    spot = lax.broadcasted_iota(jnp.int32, (KEPT, 16, DH), 1)
    rows = pl.ds(pl.multiple_of(tile, 16), 16)
    old = in_ref[:, half, rows, :].astype(jnp.float32)
    new = jnp.where(spot == within - tile, jnp.broadcast_to(row[:, None], old.shape), old)
    out_ref[:, half, rows, :] = new.astype(jnp.bfloat16)


def on_device(queries, key_rows, value_rows, rel_bias, offsets):
    bf16, f32 = jnp.bfloat16, jnp.float32
    given = (queries, key_rows, value_rows, offsets)
    packed, picks = pl.pallas_call(
        pack_kernel,
        out_shape=(
            jax.ShapeDtypeStruct((PEERS, 3 * ROWS, DH), bf16),
            jax.ShapeDtypeStruct(offsets.shape, offsets.dtype),
        ),
        in_specs=[HBM] * 4,
        out_specs=(VMEM, VMEM),
        scratch_shapes=[pltpu.SemaphoreType.DMA((4,))],
        compiler_params=params(),
        name="pack",
    )(*(pltpu.with_memory_space_constraint(t, pltpu.HBM) for t in given))
    is_low = lax.axis_index("z") < HALF
    packed, is_low = lax.optimization_barrier((packed, is_low))
    qkv = lax.all_to_all(packed, ("g", "x"), 0, 0, axis_index_groups=[ORDER_IN], tiled=True)
    kept = pl.pallas_call(
        kept_kernel,
        out_shape=jax.ShapeDtypeStruct((HALF, 2 * KEPT, DH), bf16),
        in_specs=[VMEM, VMEM],
        out_specs=VMEM,
        compiler_params=params(),
        name="kept",
    )(picks, qkv.reshape(KEPT, 2, 3 * ROWS, DH))
    def exchange(block):
        return lax.all_to_all(block, "z", 0, 0, axis_index_groups=[LOW, HIGH], tiled=True)

    def local(qkv, rel_bias):
        near_bias, mid_bias, far_bias = pl.pallas_call(
            bias_kernel,
            out_shape=(
                jax.ShapeDtypeStruct((SPAN, SPAN), f32),
                jax.ShapeDtypeStruct((SPAN, SPAN), f32),
                jax.ShapeDtypeStruct((KEPT, SPAN), f32),
            ),
            in_specs=[SMEM],
            out_specs=(VMEM, VMEM, VMEM),
            compiler_params=params(),
            name="bias",
        )(rel_bias)
        rows, far_parts = pl.pallas_call(
            local_kernel,
            out_shape=(
                jax.ShapeDtypeStruct((PEERS, ROWS, DH), bf16),
                jax.ShapeDtypeStruct((4, KEPT, DH), f32),
            ),
            in_specs=[VMEM] * 4,
            out_specs=(VMEM, VMEM),
            scratch_shapes=[
                pltpu.VMEM((3, SEG, DH), f32),
                pltpu.VMEM((SEG, DH), f32),
                pltpu.VMEM((SEG, DH), f32),
                pltpu.VMEM((SEG, DH), f32),
            ],
            compiler_params=params(),
            name="local",
        )(picks, qkv, near_bias, mid_bias)
        return rows, far_parts, far_bias

    def finish(rows, far_parts, far_bias, *kv):
        merged = pl.pallas_call(
            far_kernel,
            out_shape=jax.ShapeDtypeStruct((KEPT, 2, ROWS, DH), bf16),
            in_specs=[VMEM] * (4 + len(kv)),
            out_specs=VMEM,
            input_output_aliases={3 + len(kv): 0},
            compiler_params=params(),
            name="far",
        )(picks, far_bias, far_parts, *kv, rows.reshape(KEPT, 2, ROWS, DH))
        return lax.all_to_all(
            merged.reshape(PEERS, ROWS, DH),
            ("g", "x"),
            0,
            0,
            axis_index_groups=[ORDER_OUT],
            tiled=True,
        )

    first, *parts = lax.cond(
        is_low,
        lambda block, *rest: (exchange(block), *local(*rest)),
        lambda block, *rest: (block, *local(*rest)),
        kept,
        qkv,
        rel_bias,
    )
    lower = lax.ppermute(first, "z", [(z, PLANES - 1 - z) for z in range(HALF)])
    later = lax.cond(
        is_low,
        lambda first, kept, *parts: finish(*parts, first),
        lambda first, kept, *parts: jnp.pad(exchange(kept), ((0, PEERS - HALF), (0, 0), (0, 0))),
        first,
        kept,
        *parts,
    )
    back = lax.cond(
        is_low,
        lambda later, lower, *parts: later,
        lambda later, lower, *parts: finish(*parts, later[:HALF], lower),
        later,
        lower,
        *parts,
    )
    return pl.pallas_call(
        unpack_kernel,
        out_shape=jax.ShapeDtypeStruct((ROWS, PEERS * DH), bf16),
        in_specs=[VMEM],
        out_specs=VMEM,
        compiler_params=params(),
        name="unpack",
    )(back)


def solution(mesh):
    mesh = Mesh(mesh.devices.reshape(PLANES, GROUPS, LANES), ("z", "g", "x"))
    rows = P(("z", "g", "x"), None)
    return jax.shard_map(
        on_device,
        mesh=mesh,
        in_specs=(rows, rows, rows, P(None, "x"), P(None, "x")),
        out_specs=rows,
        check_vma=False,
    )
```

```python
import math

import jax
import jax.numpy as jnp
from jax import lax
from jax.experimental import pallas as pl
from jax.experimental.pallas import tpu as pltpu
from jax.sharding import Mesh, PartitionSpec as P

DH = 128
BUCKETS = 32
MAXDIST = 128
R1 = 4
R2 = 64
SPAN = 256
PLANES = 16
GROUPS = 8
LANES = 4
PEERS = GROUPS * LANES
ROWS = 32
SEG = PEERS * ROWS
KEPT = SEG // R2
HALF = PLANES // 2
LOW = [5, 0, 1, 2, 3, 4, 6, 7]
HIGH = [11, 8, 9, 10, 12, 13, 14, 15]
ORDER_IN = [(2 * y + c) * LANES + x for c in (0, 1) for y in (3, 2, 1, 0) for x in (3, 2, 1, 0)]
ORDER_OUT = [(2 * y + c) * LANES + x for c in (0, 1) for y in (0, 1, 2, 3) for x in (0, 1, 2, 3)]
PAIRS_IN = [n // 2 for n in ORDER_IN[::2]]
PAIRS_OUT = [n // 2 for n in ORDER_OUT[::2]]
PLACE = {n: p for p, n in enumerate(ORDER_IN)}
NEG = -1e30
SCALE = DH ** (-0.5)

VMEM = pl.BlockSpec(memory_space=pltpu.VMEM)
SMEM = pl.BlockSpec(memory_space=pltpu.SMEM)
HBM = pl.BlockSpec(memory_space=pltpu.HBM)


def params():
    return pltpu.CompilerParams(vmem_limit_bytes=24 * 1024 * 1024)


def bucket_starts():
    half = BUCKETS // 2
    starts = list(range(half + 1))
    for target in range(half + 1, BUCKETS):
        starts.append(int(math.ceil(half * (MAXDIST / half) ** ((target - half) / half))))
    return starts


def pack_kernel(
    q_ref, k_ref, v_ref, offsets_ref, bias_ref, _, out_ref, picks_ref, table_ref, sems
):
    copies = [
        pltpu.make_async_copy(offsets_ref, picks_ref, sems.at[3]),
        pltpu.make_async_copy(bias_ref, table_ref, sems.at[4]),
    ]
    for n, ref in enumerate((q_ref, k_ref, v_ref)):
        for g in range(GROUPS):
            for x in range(LANES):
                p, h = PLACE[g * LANES + x], GROUPS * x + g
                copies.append(
                    pltpu.make_async_copy(
                        ref.at[:, h * DH : (h + 1) * DH],
                        out_ref.at[p, n * ROWS : (n + 1) * ROWS],
                        sems.at[n],
                    )
                )
    for copy in copies:
        copy.start()
    for copy in copies:
        copy.wait()


def offset_of(ref, row):
    values = ref[...]
    at_row = lax.broadcasted_iota(jnp.int32, values.shape, 0) == row
    at_head = lax.broadcasted_iota(jnp.int32, values.shape, 1) == lax.axis_index("g")
    return jnp.sum(jnp.where(at_row & at_head, values, 0))


def unpack_kernel(in_ref, out_ref):
    for p, n in enumerate(ORDER_OUT):
        h = GROUPS * (n % LANES) + n // LANES
        out_ref[:, h * DH : (h + 1) * DH] = in_ref[p]


def bias_kernel(table_ref, near_ref, mid_ref, far_ref):
    starts = bucket_starts()
    head = lax.axis_index("g")
    width = 2 * SPAN
    lane = lax.broadcasted_iota(jnp.int32, (8, width), 1)
    steps = jnp.where(lane == 0, 0, width - lane)

    def value_at(distance):
        value = jnp.full(distance.shape, table_ref[head, 0], jnp.float32)
        for n in range(1, BUCKETS):
            value = jnp.where(distance >= starts[n], table_ref[head, n], value)
        return value

    def line(stride):
        return jnp.where((lane == 0) | (lane > SPAN), value_at(steps * stride), NEG)

    def spread(row, count):
        wide = jnp.broadcast_to(row[0:1], (count, width))
        return pltpu.roll(wide, 0, 1, stride=1, stride_axis=0)[:, :SPAN]

    near_ref[...] = spread(line(1), SPAN)
    mid_ref[...] = spread(line(R1), SPAN)
    row = lax.broadcasted_iota(jnp.int32, (KEPT, SPAN), 0)
    column = lax.broadcasted_iota(jnp.int32, (KEPT, SPAN), 1)
    here = lax.axis_index("z")
    plane = jnp.full((KEPT, SPAN), PLANES, jnp.int32)
    for n in range(HALF):
        own = jnp.where(here < HALF, LOW[n], HIGH[n])
        other = jnp.where(here < HALF, PLANES, LOW[n])
        plane = jnp.where(column // KEPT == n, own, plane)
        plane = jnp.where(column // KEPT == n + HALF, other, plane)
    query, key = jnp.zeros((KEPT, SPAN), jnp.int32), jnp.zeros((KEPT, SPAN), jnp.int32)
    for n in range(KEPT):
        query = jnp.where(row == n, PAIRS_OUT[n], query)
        key = jnp.where(column % KEPT == n, PAIRS_IN[n], key)
    apart = (here - plane) * KEPT + query - key
    far_ref[...] = jnp.where(apart >= 0, value_at(apart * R2), NEG)


def kept_tile(ref, part, pick):
    half = pick // ROWS
    within = pick % ROWS
    tile = (within // 16) * 16
    rows = ref[:, 1 - half, pl.ds(pl.multiple_of(part * ROWS + tile, 16), 16), :]
    spot = lax.broadcasted_iota(jnp.int32, (KEPT, 16, DH), 1)
    return jnp.sum(jnp.where(spot == within - tile, rows.astype(jnp.float32), 0.0), axis=1)


def kept_kernel(offsets_ref, qkv_ref, out_ref):
    pick = offset_of(offsets_ref, 1)
    keys = kept_tile(qkv_ref, 1, pick).astype(jnp.bfloat16)
    values = kept_tile(qkv_ref, 2, pick).astype(jnp.bfloat16)
    for z in range(HALF):
        out_ref[z, 0:KEPT] = keys
        out_ref[z, KEPT : 2 * KEPT] = values


def branch(q, k, v, bias):
    scores = lax.dot_general(
        q, k, (((1,), (1,)), ((), ())), preferred_element_type=jnp.float32
    ) * SCALE + bias
    top = jnp.max(scores, axis=1, keepdims=True)
    weight = jnp.exp(scores - top)
    total = jnp.sum(weight, axis=1, keepdims=True)
    acc = jnp.dot(weight.astype(jnp.bfloat16), v, preferred_element_type=jnp.float32)
    shape = acc.shape
    return acc, jnp.broadcast_to(top, shape), jnp.broadcast_to(total, shape)


def merge(one, two):
    acc1, top1, total1 = one
    acc2, top2, total2 = two
    top = jnp.maximum(top1, top2)
    w1, w2 = jnp.exp(top1 - top), jnp.exp(top2 - top)
    return acc1 * w1 + acc2 * w2, top, total1 * w1 + total2 * w2


def local_kernel(
    offsets_ref, qkv_ref, near_ref, mid_ref, out_ref, far_ref, wide, acc_ref, top_ref, total_ref
):
    near_bias = near_ref[...]
    count = SPAN // ROWS
    for s in range(SEG // SPAN):
        blocks = [PLACE[n] for n in range(s * count, (s + 1) * count)]
        rows = slice(s * SPAN, (s + 1) * SPAN)
        q, k, v = (
            jnp.concatenate([qkv_ref[p, n * ROWS : (n + 1) * ROWS] for p in blocks], axis=0)
            for n in range(3)
        )
        wide[0, rows] = q.astype(jnp.float32)
        wide[1, rows] = k.astype(jnp.float32)
        wide[2, rows] = v.astype(jnp.float32)
        acc_ref[rows], top_ref[rows], total_ref[rows] = branch(q, k, v, near_bias)
    kept = pl.ds(offset_of(offsets_ref, 0), SPAN, stride=R1)
    q, k, v = (wide[n, kept, :].astype(jnp.bfloat16) for n in range(3))
    mid = branch(q, k, v, mid_ref[...])
    merged = merge((acc_ref[kept, :], top_ref[kept, :], total_ref[kept, :]), mid)
    acc_ref[kept, :], top_ref[kept, :], total_ref[kept, :] = merged
    for p, n in enumerate(ORDER_OUT):
        rows = slice(n * ROWS, (n + 1) * ROWS)
        out_ref[p] = (acc_ref[rows] / total_ref[rows]).astype(jnp.bfloat16)
    far = pl.ds(offset_of(offsets_ref, 1), KEPT, stride=R2)
    parts = acc_ref[far, :], top_ref[far, :], total_ref[far, :], wide[0, far, :]
    for n, part in enumerate(parts):
        for m, pair in enumerate(PAIRS_OUT):
            far_ref[n, m : m + 1] = part[pair : pair + 1]


def far_kernel(offsets_ref, bias_ref, far_ref, *refs):
    *kv_refs, in_ref, out_ref = refs
    q = far_ref[3].astype(jnp.bfloat16)
    kv = jnp.concatenate([ref[...] for ref in kv_refs], axis=0)
    count = kv.shape[0] * KEPT
    k = kv[:, 0:KEPT].reshape(count, DH)
    v = kv[:, KEPT : 2 * KEPT].reshape(count, DH)
    far = branch(q, k, v, bias_ref[:, 0:count])
    acc, _, total = merge((far_ref[0], far_ref[1], far_ref[2]), far)
    row = (acc / total).astype(jnp.bfloat16).astype(jnp.float32)
    out_ref[...] = in_ref[...]
    pick = offset_of(offsets_ref, 1)
    half = pick // ROWS
    within = pick % ROWS
    tile = (within // 16) * 16
    spot = lax.broadcasted_iota(jnp.int32, (KEPT, 16, DH), 1)
    rows = pl.ds(pl.multiple_of(tile, 16), 16)
    old = in_ref[:, half, rows, :].astype(jnp.float32)
    new = jnp.where(spot == within - tile, jnp.broadcast_to(row[:, None], old.shape), old)
    out_ref[:, half, rows, :] = new.astype(jnp.bfloat16)


def on_device(queries, key_rows, value_rows, rel_bias, offsets):
    bf16, f32 = jnp.bfloat16, jnp.float32
    is_low = lax.axis_index("z") < HALF
    given = (queries, key_rows, value_rows, offsets, rel_bias.T, is_low.astype(jnp.int32)[None])
    packed, picks, table = pl.pallas_call(
        pack_kernel,
        out_shape=(
            jax.ShapeDtypeStruct((PEERS, 3 * ROWS, DH), bf16),
            jax.ShapeDtypeStruct(offsets.shape, offsets.dtype),
            jax.ShapeDtypeStruct(rel_bias.T.shape, f32),
        ),
        in_specs=[HBM] * 6,
        out_specs=(VMEM, VMEM, VMEM),
        scratch_shapes=[pltpu.SemaphoreType.DMA((5,))],
        compiler_params=params(),
        name="pack",
    )(*(pltpu.with_memory_space_constraint(t, pltpu.HBM) for t in given))
    qkv = lax.all_to_all(packed, ("g", "x"), 0, 0, axis_index_groups=[ORDER_IN], tiled=True)
    kept = pl.pallas_call(
        kept_kernel,
        out_shape=jax.ShapeDtypeStruct((HALF, 2 * KEPT, DH), bf16),
        in_specs=[VMEM, VMEM],
        out_specs=VMEM,
        compiler_params=params(),
        name="kept",
    )(picks, qkv.reshape(KEPT, 2, 3 * ROWS, DH))
    def exchange(block):
        return lax.all_to_all(block, "z", 0, 0, axis_index_groups=[LOW, HIGH], tiled=True)

    def local(qkv, table):
        near_bias, mid_bias, far_bias = pl.pallas_call(
            bias_kernel,
            out_shape=(
                jax.ShapeDtypeStruct((SPAN, SPAN), f32),
                jax.ShapeDtypeStruct((SPAN, SPAN), f32),
                jax.ShapeDtypeStruct((KEPT, SPAN), f32),
            ),
            in_specs=[SMEM],
            out_specs=(VMEM, VMEM, VMEM),
            compiler_params=params(),
            name="bias",
        )(table)
        rows, far_parts = pl.pallas_call(
            local_kernel,
            out_shape=(
                jax.ShapeDtypeStruct((PEERS, ROWS, DH), bf16),
                jax.ShapeDtypeStruct((4, KEPT, DH), f32),
            ),
            in_specs=[VMEM] * 4,
            out_specs=(VMEM, VMEM),
            scratch_shapes=[
                pltpu.VMEM((3, SEG, DH), f32),
                pltpu.VMEM((SEG, DH), f32),
                pltpu.VMEM((SEG, DH), f32),
                pltpu.VMEM((SEG, DH), f32),
            ],
            compiler_params=params(),
            name="local",
        )(picks, qkv, near_bias, mid_bias)
        return rows, far_parts, far_bias

    def finish(rows, far_parts, far_bias, *kv):
        merged = pl.pallas_call(
            far_kernel,
            out_shape=jax.ShapeDtypeStruct((KEPT, 2, ROWS, DH), bf16),
            in_specs=[VMEM] * (4 + len(kv)),
            out_specs=VMEM,
            input_output_aliases={3 + len(kv): 0},
            compiler_params=params(),
            name="far",
        )(picks, far_bias, far_parts, *kv, rows.reshape(KEPT, 2, ROWS, DH))
        return lax.all_to_all(
            merged.reshape(PEERS, ROWS, DH),
            ("g", "x"),
            0,
            0,
            axis_index_groups=[ORDER_OUT],
            tiled=True,
        )

    first, *parts = lax.cond(
        is_low,
        lambda block, *rest: (exchange(block), *local(*rest)),
        lambda block, *rest: (jnp.zeros_like(block), *local(*rest)),
        kept,
        qkv,
        table,
    )
    lower = lax.ppermute(first, "z", [(z, PLANES - 1 - z) for z in range(HALF)])
    later = lax.cond(
        is_low,
        lambda first, kept, *parts: finish(*parts, first),
        lambda first, kept, *parts: jnp.pad(exchange(kept), ((0, PEERS - HALF), (0, 0), (0, 0))),
        first,
        kept,
        *parts,
    )
    back = lax.cond(
        is_low,
        lambda later, lower, *parts: later,
        lambda later, lower, *parts: finish(*parts, later[:HALF], lower),
        later,
        lower,
        *parts,
    )
    return pl.pallas_call(
        unpack_kernel,
        out_shape=jax.ShapeDtypeStruct((ROWS, PEERS * DH), bf16),
        in_specs=[VMEM],
        out_specs=VMEM,
        compiler_params=params(),
        name="unpack",
    )(back)


def solution(mesh):
    mesh = Mesh(mesh.devices.reshape(PLANES, GROUPS, LANES), ("z", "g", "x"))
    rows = P(("z", "g", "x"), None)
    return jax.shard_map(
        on_device,
        mesh=mesh,
        in_specs=(rows, rows, rows, P(None, "x"), P(None, "x")),
        out_specs=rows,
        check_vma=False,
    )
```

```python
import math

import jax
import jax.numpy as jnp
from jax import lax
from jax.experimental import pallas as pl
from jax.experimental.pallas import tpu as pltpu
from jax.sharding import Mesh, PartitionSpec as P

DH = 128
BUCKETS = 32
MAXDIST = 128
R1 = 4
R2 = 64
SPAN = 256
PLANES = 16
GROUPS = 8
LANES = 4
PEERS = GROUPS * LANES
ROWS = 32
SEG = PEERS * ROWS
KEPT = SEG // R2
HALF = PLANES // 2
LOW = [6, 0, 1, 2, 3, 4, 5, 7]
HIGH = [11, 8, 9, 10, 12, 13, 14, 15]
ORDER_IN = [(2 * y + c) * LANES + x for c in (1, 0) for y in (3, 2, 1, 0) for x in (3, 2, 1, 0)]
ORDER_OUT = [(2 * y + c) * LANES + x for c in (0, 1) for y in (0, 1, 2, 3) for x in (0, 1, 2, 3)]
PAIRS_IN = [n // 2 for n in ORDER_IN[::2]]
PAIRS_OUT = [n // 2 for n in ORDER_OUT[::2]]
PLACE = {n: p for p, n in enumerate(ORDER_IN)}
UPPER = [12, 13, 14, 15, 11, 10, 8, 9]
NEG = -1e30
SCALE = DH ** (-0.5)

VMEM = pl.BlockSpec(memory_space=pltpu.VMEM)
SMEM = pl.BlockSpec(memory_space=pltpu.SMEM)
HBM = pl.BlockSpec(memory_space=pltpu.HBM)


def params():
    return pltpu.CompilerParams(vmem_limit_bytes=24 * 1024 * 1024)


def bucket_starts():
    half = BUCKETS // 2
    starts = list(range(half + 1))
    for target in range(half + 1, BUCKETS):
        starts.append(int(math.ceil(half * (MAXDIST / half) ** ((target - half) / half))))
    return starts


def pack_kernel(
    q_ref, k_ref, v_ref, offsets_ref, bias_ref, _, out_ref, picks_ref, table_ref, sems
):
    copies = [
        pltpu.make_async_copy(offsets_ref, picks_ref, sems.at[3]),
        pltpu.make_async_copy(bias_ref, table_ref, sems.at[4]),
    ]
    for n, ref in enumerate((q_ref, k_ref, v_ref)):
        for g in range(GROUPS):
            for x in range(LANES):
                p, h = PLACE[g * LANES + x], GROUPS * x + g
                copies.append(
                    pltpu.make_async_copy(
                        ref.at[:, h * DH : (h + 1) * DH],
                        out_ref.at[p, n * ROWS : (n + 1) * ROWS],
                        sems.at[n],
                    )
                )
    for copy in copies:
        copy.start()
    for copy in copies:
        copy.wait()


def offset_of(ref, row):
    values = ref[...]
    at_row = lax.broadcasted_iota(jnp.int32, values.shape, 0) == row
    at_head = lax.broadcasted_iota(jnp.int32, values.shape, 1) == lax.axis_index("g")
    return jnp.sum(jnp.where(at_row & at_head, values, 0))


def unpack_kernel(in_ref, out_ref):
    for p, n in enumerate(ORDER_OUT):
        h = GROUPS * (n % LANES) + n // LANES
        out_ref[:, h * DH : (h + 1) * DH] = in_ref[p]


def bias_kernel(table_ref, near_ref, mid_ref, far_ref):
    starts = bucket_starts()
    head = lax.axis_index("g")
    width = 2 * SPAN
    lane = lax.broadcasted_iota(jnp.int32, (8, width), 1)
    steps = jnp.where(lane == 0, 0, width - lane)

    def value_at(distance):
        value = jnp.full(distance.shape, table_ref[head, 0], jnp.float32)
        for n in range(1, BUCKETS):
            value = jnp.where(distance >= starts[n], table_ref[head, n], value)
        return value

    def line(stride):
        return jnp.where((lane == 0) | (lane > SPAN), value_at(steps * stride), NEG)

    def spread(row, count):
        wide = jnp.broadcast_to(row[0:1], (count, width))
        return pltpu.roll(wide, 0, 1, stride=1, stride_axis=0)[:, :SPAN]

    near_ref[...] = spread(line(1), SPAN)
    mid_ref[...] = spread(line(R1), SPAN)
    row = lax.broadcasted_iota(jnp.int32, (KEPT, SPAN), 0)
    column = lax.broadcasted_iota(jnp.int32, (KEPT, SPAN), 1)
    here = lax.axis_index("z")
    plane = jnp.full((KEPT, SPAN), PLANES, jnp.int32)
    for n in range(HALF):
        own = jnp.where(here < HALF, LOW[n], HIGH[n])
        other = jnp.where(here < HALF, PLANES, LOW[n])
        plane = jnp.where(column // KEPT == n, own, plane)
        plane = jnp.where(column // KEPT == n + HALF, other, plane)
    query, key = jnp.zeros((KEPT, SPAN), jnp.int32), jnp.zeros((KEPT, SPAN), jnp.int32)
    for n in range(KEPT):
        query = jnp.where(row == n, PAIRS_OUT[n], query)
        key = jnp.where(column % KEPT == n, PAIRS_IN[n], key)
    apart = (here - plane) * KEPT + query - key
    far_ref[...] = jnp.where(apart >= 0, value_at(apart * R2), NEG)


def kept_tile(ref, part, pick):
    half = pick // ROWS
    within = pick % ROWS
    tile = (within // 16) * 16
    rows = ref[:, 1 - half, pl.ds(pl.multiple_of(part * ROWS + tile, 16), 16), :]
    spot = lax.broadcasted_iota(jnp.int32, (KEPT, 16, DH), 1)
    return jnp.sum(jnp.where(spot == within - tile, rows.astype(jnp.float32), 0.0), axis=1)


def kept_kernel(offsets_ref, qkv_ref, out_ref):
    pick = offset_of(offsets_ref, 1)
    keys = kept_tile(qkv_ref, 1, pick).astype(jnp.bfloat16)
    values = kept_tile(qkv_ref, 2, pick).astype(jnp.bfloat16)
    for z in range(HALF):
        out_ref[z, 0:KEPT] = keys
        out_ref[z, KEPT : 2 * KEPT] = values


def branch(q, k, v, bias):
    scores = lax.dot_general(
        q, k, (((1,), (1,)), ((), ())), preferred_element_type=jnp.float32
    ) * SCALE + bias
    top = jnp.max(scores, axis=1, keepdims=True)
    weight = jnp.exp(scores - top)
    total = jnp.sum(weight, axis=1, keepdims=True)
    acc = jnp.dot(weight.astype(jnp.bfloat16), v, preferred_element_type=jnp.float32)
    shape = acc.shape
    return acc, jnp.broadcast_to(top, shape), jnp.broadcast_to(total, shape)


def merge(one, two):
    acc1, top1, total1 = one
    acc2, top2, total2 = two
    top = jnp.maximum(top1, top2)
    w1, w2 = jnp.exp(top1 - top), jnp.exp(top2 - top)
    return acc1 * w1 + acc2 * w2, top, total1 * w1 + total2 * w2


def local_kernel(
    offsets_ref, qkv_ref, near_ref, mid_ref, out_ref, far_ref, wide, acc_ref, top_ref, total_ref
):
    near_bias = near_ref[...]
    count = SPAN // ROWS
    for s in range(SEG // SPAN):
        blocks = [PLACE[n] for n in range(s * count, (s + 1) * count)]
        rows = slice(s * SPAN, (s + 1) * SPAN)
        q, k, v = (
            jnp.concatenate([qkv_ref[p, n * ROWS : (n + 1) * ROWS] for p in blocks], axis=0)
            for n in range(3)
        )
        wide[0, rows] = q.astype(jnp.float32)
        wide[1, rows] = k.astype(jnp.float32)
        wide[2, rows] = v.astype(jnp.float32)
        acc_ref[rows], top_ref[rows], total_ref[rows] = branch(q, k, v, near_bias)
    kept = pl.ds(offset_of(offsets_ref, 0), SPAN, stride=R1)
    q, k, v = (wide[n, kept, :].astype(jnp.bfloat16) for n in range(3))
    mid = branch(q, k, v, mid_ref[...])
    merged = merge((acc_ref[kept, :], top_ref[kept, :], total_ref[kept, :]), mid)
    acc_ref[kept, :], top_ref[kept, :], total_ref[kept, :] = merged
    for p, n in enumerate(ORDER_OUT):
        rows = slice(n * ROWS, (n + 1) * ROWS)
        out_ref[p] = (acc_ref[rows] / total_ref[rows]).astype(jnp.bfloat16)
    far = pl.ds(offset_of(offsets_ref, 1), KEPT, stride=R2)
    parts = acc_ref[far, :], top_ref[far, :], total_ref[far, :], wide[0, far, :]
    for n, part in enumerate(parts):
        for m, pair in enumerate(PAIRS_OUT):
            far_ref[n, m : m + 1] = part[pair : pair + 1]


def far_kernel(offsets_ref, bias_ref, far_ref, *refs):
    *kv_refs, in_ref, out_ref = refs
    q = far_ref[3].astype(jnp.bfloat16)
    kv = jnp.concatenate([ref[...] for ref in kv_refs], axis=0)
    count = kv.shape[0] * KEPT
    k = kv[:, 0:KEPT].reshape(count, DH)
    v = kv[:, KEPT : 2 * KEPT].reshape(count, DH)
    far = branch(q, k, v, bias_ref[:, 0:count])
    acc, _, total = merge((far_ref[0], far_ref[1], far_ref[2]), far)
    row = (acc / total).astype(jnp.bfloat16).astype(jnp.float32)
    out_ref[...] = in_ref[...]
    pick = offset_of(offsets_ref, 1)
    half = pick // ROWS
    within = pick % ROWS
    tile = (within // 16) * 16
    spot = lax.broadcasted_iota(jnp.int32, (KEPT, 16, DH), 1)
    rows = pl.ds(pl.multiple_of(tile, 16), 16)
    old = in_ref[:, half, rows, :].astype(jnp.float32)
    new = jnp.where(spot == within - tile, jnp.broadcast_to(row[:, None], old.shape), old)
    out_ref[:, half, rows, :] = new.astype(jnp.bfloat16)


def on_device(queries, key_rows, value_rows, rel_bias, offsets):
    bf16, f32 = jnp.bfloat16, jnp.float32
    is_low = lax.axis_index("z") < HALF
    given = (queries, key_rows, value_rows, offsets, rel_bias.T, is_low.astype(jnp.int32)[None])
    packed, picks, table = pl.pallas_call(
        pack_kernel,
        out_shape=(
            jax.ShapeDtypeStruct((PEERS, 3 * ROWS, DH), bf16),
            jax.ShapeDtypeStruct(offsets.shape, offsets.dtype),
            jax.ShapeDtypeStruct(rel_bias.T.shape, f32),
        ),
        in_specs=[HBM] * 6,
        out_specs=(VMEM, VMEM, VMEM),
        scratch_shapes=[pltpu.SemaphoreType.DMA((5,))],
        compiler_params=params(),
        name="pack",
    )(*(pltpu.with_memory_space_constraint(t, pltpu.HBM) for t in given))
    qkv = lax.all_to_all(packed, ("g", "x"), 0, 0, axis_index_groups=[ORDER_IN], tiled=True)
    kept = pl.pallas_call(
        kept_kernel,
        out_shape=jax.ShapeDtypeStruct((HALF, 2 * KEPT, DH), bf16),
        in_specs=[VMEM, VMEM],
        out_specs=VMEM,
        compiler_params=params(),
        name="kept",
    )(picks, qkv.reshape(KEPT, 2, 3 * ROWS, DH))
    def exchange(block):
        return lax.all_to_all(block, "z", 0, 0, axis_index_groups=[LOW, HIGH], tiled=True)

    def local(qkv, table):
        near_bias, mid_bias, far_bias = pl.pallas_call(
            bias_kernel,
            out_shape=(
                jax.ShapeDtypeStruct((SPAN, SPAN), f32),
                jax.ShapeDtypeStruct((SPAN, SPAN), f32),
                jax.ShapeDtypeStruct((KEPT, SPAN), f32),
            ),
            in_specs=[SMEM],
            out_specs=(VMEM, VMEM, VMEM),
            compiler_params=params(),
            name="bias",
        )(table)
        rows, far_parts = pl.pallas_call(
            local_kernel,
            out_shape=(
                jax.ShapeDtypeStruct((PEERS, ROWS, DH), bf16),
                jax.ShapeDtypeStruct((4, KEPT, DH), f32),
            ),
            in_specs=[VMEM] * 4,
            out_specs=(VMEM, VMEM),
            scratch_shapes=[
                pltpu.VMEM((3, SEG, DH), f32),
                pltpu.VMEM((SEG, DH), f32),
                pltpu.VMEM((SEG, DH), f32),
                pltpu.VMEM((SEG, DH), f32),
            ],
            compiler_params=params(),
            name="local",
        )(picks, qkv, near_bias, mid_bias)
        return rows, far_parts, far_bias

    def finish(rows, far_parts, far_bias, *kv):
        merged = pl.pallas_call(
            far_kernel,
            out_shape=jax.ShapeDtypeStruct((KEPT, 2, ROWS, DH), bf16),
            in_specs=[VMEM] * (4 + len(kv)),
            out_specs=VMEM,
            input_output_aliases={3 + len(kv): 0},
            compiler_params=params(),
            name="far",
        )(picks, far_bias, far_parts, *kv, rows.reshape(KEPT, 2, ROWS, DH))
        return lax.all_to_all(
            merged.reshape(PEERS, ROWS, DH),
            ("g", "x"),
            0,
            0,
            axis_index_groups=[ORDER_OUT],
            tiled=True,
        )

    first, *parts = lax.cond(
        is_low,
        lambda block, *rest: (exchange(block), *local(*rest)),
        lambda block, *rest: (jnp.zeros_like(block), *local(*rest)),
        kept,
        qkv,
        table,
    )
    lower = lax.ppermute(first, "z", list(enumerate(UPPER)))
    later = lax.cond(
        is_low,
        lambda first, kept, *parts: finish(*parts, first),
        lambda first, kept, *parts: jnp.pad(exchange(kept), ((0, PEERS - HALF), (0, 0), (0, 0))),
        first,
        kept,
        *parts,
    )
    back = lax.cond(
        is_low,
        lambda later, lower, *parts: later,
        lambda later, lower, *parts: finish(*parts, later[:HALF], lower),
        later,
        lower,
        *parts,
    )
    return pl.pallas_call(
        unpack_kernel,
        out_shape=jax.ShapeDtypeStruct((ROWS, PEERS * DH), bf16),
        in_specs=[VMEM],
        out_specs=VMEM,
        compiler_params=params(),
        name="unpack",
    )(back)


def solution(mesh):
    mesh = Mesh(mesh.devices.reshape(PLANES, GROUPS, LANES), ("z", "g", "x"))
    rows = P(("z", "g", "x"), None)
    return jax.shard_map(
        on_device,
        mesh=mesh,
        in_specs=(rows, rows, rows, P(None, "x"), P(None, "x")),
        out_specs=rows,
        check_vma=False,
    )
```

```python
import math

import jax
import jax.numpy as jnp
from jax import lax
from jax.experimental import pallas as pl
from jax.experimental.pallas import tpu as pltpu
from jax.sharding import Mesh, PartitionSpec as P

DH = 128
BUCKETS = 32
MAXDIST = 128
R1 = 4
R2 = 64
SPAN = 256
PLANES = 16
GROUPS = 8
LANES = 4
PEERS = GROUPS * LANES
ROWS = 32
SEG = PEERS * ROWS
KEPT = SEG // R2
HALF = PLANES // 2
LOW = [6, 0, 1, 2, 3, 4, 5, 7]
HIGH = [11, 8, 9, 10, 12, 13, 14, 15]
ORDER_IN = [(2 * y + c) * LANES + x for c in (1, 0) for y in (3, 2, 1, 0) for x in (3, 2, 1, 0)]
ORDER_OUT = [(2 * y + c) * LANES + x for c in (1, 0) for y in (0, 1, 2, 3) for x in (0, 1, 2, 3)]
PAIRS_IN = [n // 2 for n in ORDER_IN[::2]]
PAIRS_OUT = [n // 2 for n in ORDER_OUT[::2]]
PLACE = {n: p for p, n in enumerate(ORDER_IN)}
UPPER = [12, 13, 14, 15, 11, 10, 8, 9]
NEG = -1e30
SCALE = DH ** (-0.5)

VMEM = pl.BlockSpec(memory_space=pltpu.VMEM)
SMEM = pl.BlockSpec(memory_space=pltpu.SMEM)
HBM = pl.BlockSpec(memory_space=pltpu.HBM)


def params():
    return pltpu.CompilerParams(vmem_limit_bytes=24 * 1024 * 1024)


def bucket_starts():
    half = BUCKETS // 2
    starts = list(range(half + 1))
    for target in range(half + 1, BUCKETS):
        starts.append(int(math.ceil(half * (MAXDIST / half) ** ((target - half) / half))))
    return starts


def pack_kernel(
    q_ref, k_ref, v_ref, offsets_ref, bias_ref, _, out_ref, picks_ref, table_ref, __, sems
):
    copies = [
        pltpu.make_async_copy(offsets_ref, picks_ref, sems.at[3]),
        pltpu.make_async_copy(bias_ref, table_ref, sems.at[4]),
    ]
    for n, ref in enumerate((q_ref, k_ref, v_ref)):
        for g in range(GROUPS):
            for x in range(LANES):
                p, h = PLACE[g * LANES + x], GROUPS * x + g
                copies.append(
                    pltpu.make_async_copy(
                        ref.at[:, h * DH : (h + 1) * DH],
                        out_ref.at[p, n * ROWS : (n + 1) * ROWS],
                        sems.at[n],
                    )
                )
    for copy in copies:
        copy.start()
    for copy in copies:
        copy.wait()


def offset_of(ref, row):
    values = ref[...]
    at_row = lax.broadcasted_iota(jnp.int32, values.shape, 0) == row
    at_head = lax.broadcasted_iota(jnp.int32, values.shape, 1) == lax.axis_index("g")
    return jnp.sum(jnp.where(at_row & at_head, values, 0))


def unpack_kernel(in_ref, out_ref):
    for p, n in enumerate(ORDER_OUT):
        h = GROUPS * (n % LANES) + n // LANES
        out_ref[:, h * DH : (h + 1) * DH] = in_ref[p]


def bias_kernel(table_ref, near_ref, mid_ref, far_ref):
    starts = bucket_starts()
    head = lax.axis_index("g")
    width = 2 * SPAN
    lane = lax.broadcasted_iota(jnp.int32, (8, width), 1)
    steps = jnp.where(lane == 0, 0, width - lane)

    def value_at(distance):
        value = jnp.full(distance.shape, table_ref[head, 0], jnp.float32)
        for n in range(1, BUCKETS):
            value = jnp.where(distance >= starts[n], table_ref[head, n], value)
        return value

    def line(stride):
        return jnp.where((lane == 0) | (lane > SPAN), value_at(steps * stride), NEG)

    def spread(row, count):
        wide = jnp.broadcast_to(row[0:1], (count, width))
        return pltpu.roll(wide, 0, 1, stride=1, stride_axis=0)[:, :SPAN]

    near_ref[...] = spread(line(1), SPAN)
    mid_ref[...] = spread(line(R1), SPAN)
    row = lax.broadcasted_iota(jnp.int32, (KEPT, SPAN), 0)
    column = lax.broadcasted_iota(jnp.int32, (KEPT, SPAN), 1)
    here = lax.axis_index("z")
    plane = jnp.full((KEPT, SPAN), PLANES, jnp.int32)
    for n in range(HALF):
        own = jnp.where(here < HALF, LOW[n], HIGH[n])
        other = jnp.where(here < HALF, PLANES, LOW[n])
        plane = jnp.where(column // KEPT == n, own, plane)
        plane = jnp.where(column // KEPT == n + HALF, other, plane)
    query, key = jnp.zeros((KEPT, SPAN), jnp.int32), jnp.zeros((KEPT, SPAN), jnp.int32)
    for n in range(KEPT):
        query = jnp.where(row == n, PAIRS_OUT[n], query)
        key = jnp.where(column % KEPT == n, PAIRS_IN[n], key)
    apart = (here - plane) * KEPT + query - key
    far_ref[...] = jnp.where(apart >= 0, value_at(apart * R2), NEG)


def kept_tile(ref, part, pick):
    half = pick // ROWS
    within = pick % ROWS
    tile = (within // 16) * 16
    rows = ref[:, 1 - half, pl.ds(pl.multiple_of(part * ROWS + tile, 16), 16), :]
    spot = lax.broadcasted_iota(jnp.int32, (KEPT, 16, DH), 1)
    return jnp.sum(jnp.where(spot == within - tile, rows.astype(jnp.float32), 0.0), axis=1)


def kept_kernel(offsets_ref, qkv_ref, out_ref):
    pick = offset_of(offsets_ref, 1)
    keys = kept_tile(qkv_ref, 1, pick).astype(jnp.bfloat16)
    values = kept_tile(qkv_ref, 2, pick).astype(jnp.bfloat16)
    for z in range(HALF):
        out_ref[z, 0:KEPT] = keys
        out_ref[z, KEPT : 2 * KEPT] = values


def branch(q, k, v, bias):
    scores = lax.dot_general(
        q, k, (((1,), (1,)), ((), ())), preferred_element_type=jnp.float32
    ) * SCALE + bias
    top = jnp.max(scores, axis=1, keepdims=True)
    weight = jnp.exp(scores - top)
    total = jnp.sum(weight, axis=1, keepdims=True)
    acc = jnp.dot(weight.astype(jnp.bfloat16), v, preferred_element_type=jnp.float32)
    shape = acc.shape
    return acc, jnp.broadcast_to(top, shape), jnp.broadcast_to(total, shape)


def merge(one, two):
    acc1, top1, total1 = one
    acc2, top2, total2 = two
    top = jnp.maximum(top1, top2)
    w1, w2 = jnp.exp(top1 - top), jnp.exp(top2 - top)
    return acc1 * w1 + acc2 * w2, top, total1 * w1 + total2 * w2


def local_kernel(
    offsets_ref, qkv_ref, near_ref, mid_ref, out_ref, far_ref, wide, acc_ref, top_ref, total_ref
):
    near_bias = near_ref[...]
    count = SPAN // ROWS
    for s in range(SEG // SPAN):
        blocks = [PLACE[n] for n in range(s * count, (s + 1) * count)]
        rows = slice(s * SPAN, (s + 1) * SPAN)
        q, k, v = (
            jnp.concatenate([qkv_ref[p, n * ROWS : (n + 1) * ROWS] for p in blocks], axis=0)
            for n in range(3)
        )
        wide[0, rows] = q.astype(jnp.float32)
        wide[1, rows] = k.astype(jnp.float32)
        wide[2, rows] = v.astype(jnp.float32)
        acc_ref[rows], top_ref[rows], total_ref[rows] = branch(q, k, v, near_bias)
    kept = pl.ds(offset_of(offsets_ref, 0), SPAN, stride=R1)
    q, k, v = (wide[n, kept, :].astype(jnp.bfloat16) for n in range(3))
    mid = branch(q, k, v, mid_ref[...])
    merged = merge((acc_ref[kept, :], top_ref[kept, :], total_ref[kept, :]), mid)
    acc_ref[kept, :], top_ref[kept, :], total_ref[kept, :] = merged
    for p, n in enumerate(ORDER_OUT):
        rows = slice(n * ROWS, (n + 1) * ROWS)
        out_ref[p] = (acc_ref[rows] / total_ref[rows]).astype(jnp.bfloat16)
    far = pl.ds(offset_of(offsets_ref, 1), KEPT, stride=R2)
    parts = acc_ref[far, :], top_ref[far, :], total_ref[far, :], wide[0, far, :]
    for n, part in enumerate(parts):
        for m, pair in enumerate(PAIRS_OUT):
            far_ref[n, m : m + 1] = part[pair : pair + 1]


def far_kernel(offsets_ref, bias_ref, far_ref, *refs):
    *kv_refs, in_ref, out_ref = refs
    q = far_ref[3].astype(jnp.bfloat16)
    kv = jnp.concatenate([ref[...] for ref in kv_refs], axis=0)
    count = kv.shape[0] * KEPT
    k = kv[:, 0:KEPT].reshape(count, DH)
    v = kv[:, KEPT : 2 * KEPT].reshape(count, DH)
    far = branch(q, k, v, bias_ref[:, 0:count])
    acc, _, total = merge((far_ref[0], far_ref[1], far_ref[2]), far)
    row = (acc / total).astype(jnp.bfloat16).astype(jnp.float32)
    out_ref[...] = in_ref[...]
    pick = offset_of(offsets_ref, 1)
    half = pick // ROWS
    within = pick % ROWS
    tile = (within // 16) * 16
    spot = lax.broadcasted_iota(jnp.int32, (KEPT, 16, DH), 1)
    rows = pl.ds(pl.multiple_of(tile, 16), 16)
    old = in_ref[:, half, rows, :].astype(jnp.float32)
    new = jnp.where(spot == within - tile, jnp.broadcast_to(row[:, None], old.shape), old)
    out_ref[:, half, rows, :] = new.astype(jnp.bfloat16)


def on_device(queries, key_rows, value_rows, rel_bias, offsets):
    bf16, f32 = jnp.bfloat16, jnp.float32
    is_low = lax.axis_index("z") < HALF
    given = (queries, key_rows, value_rows, offsets, rel_bias.T, is_low.astype(jnp.int32)[None])
    packed, picks, table, spare = pl.pallas_call(
        pack_kernel,
        out_shape=(
            jax.ShapeDtypeStruct((PEERS, 3 * ROWS, DH), bf16),
            jax.ShapeDtypeStruct(offsets.shape, offsets.dtype),
            jax.ShapeDtypeStruct(rel_bias.T.shape, f32),
            jax.ShapeDtypeStruct((HALF, 2 * KEPT, DH), bf16),
        ),
        in_specs=[HBM] * 6,
        out_specs=(VMEM, VMEM, VMEM, HBM),
        scratch_shapes=[pltpu.SemaphoreType.DMA((5,))],
        compiler_params=params(),
        name="pack",
    )(*(pltpu.with_memory_space_constraint(t, pltpu.HBM) for t in given))
    qkv = lax.all_to_all(packed, ("g", "x"), 0, 0, axis_index_groups=[ORDER_IN], tiled=True)
    kept = pl.pallas_call(
        kept_kernel,
        out_shape=jax.ShapeDtypeStruct((HALF, 2 * KEPT, DH), bf16),
        in_specs=[VMEM, VMEM],
        out_specs=VMEM,
        compiler_params=params(),
        name="kept",
    )(picks, qkv.reshape(KEPT, 2, 3 * ROWS, DH))
    def exchange(block):
        return lax.all_to_all(block, "z", 0, 0, axis_index_groups=[LOW, HIGH], tiled=True)

    def local(qkv, table):
        near_bias, mid_bias, far_bias = pl.pallas_call(
            bias_kernel,
            out_shape=(
                jax.ShapeDtypeStruct((SPAN, SPAN), f32),
                jax.ShapeDtypeStruct((SPAN, SPAN), f32),
                jax.ShapeDtypeStruct((KEPT, SPAN), f32),
            ),
            in_specs=[SMEM],
            out_specs=(VMEM, VMEM, VMEM),
            compiler_params=params(),
            name="bias",
        )(table)
        rows, far_parts = pl.pallas_call(
            local_kernel,
            out_shape=(
                jax.ShapeDtypeStruct((PEERS, ROWS, DH), bf16),
                jax.ShapeDtypeStruct((4, KEPT, DH), f32),
            ),
            in_specs=[VMEM] * 4,
            out_specs=(VMEM, VMEM),
            scratch_shapes=[
                pltpu.VMEM((3, SEG, DH), f32),
                pltpu.VMEM((SEG, DH), f32),
                pltpu.VMEM((SEG, DH), f32),
                pltpu.VMEM((SEG, DH), f32),
            ],
            compiler_params=params(),
            name="local",
        )(picks, qkv, near_bias, mid_bias)
        return rows, far_parts, far_bias

    def finish(rows, far_parts, far_bias, *kv):
        merged = pl.pallas_call(
            far_kernel,
            out_shape=jax.ShapeDtypeStruct((KEPT, 2, ROWS, DH), bf16),
            in_specs=[VMEM] * (4 + len(kv)),
            out_specs=VMEM,
            input_output_aliases={3 + len(kv): 0},
            compiler_params=params(),
            name="far",
        )(picks, far_bias, far_parts, *kv, rows.reshape(KEPT, 2, ROWS, DH))
        return lax.all_to_all(
            merged.reshape(PEERS, ROWS, DH),
            ("g", "x"),
            0,
            0,
            axis_index_groups=[ORDER_OUT],
            tiled=True,
        )

    first, *parts = lax.cond(
        is_low,
        lambda block, spare, *rest: (exchange(block), *local(*rest)),
        lambda block, spare, *rest: (spare, *local(*rest)),
        kept,
        spare,
        qkv,
        table,
    )
    lower = lax.ppermute(first, "z", list(enumerate(UPPER)))
    later = lax.cond(
        is_low,
        lambda first, kept, *parts: finish(*parts, first),
        lambda first, kept, *parts: jnp.pad(exchange(kept), ((0, PEERS - HALF), (0, 0), (0, 0))),
        first,
        kept,
        *parts,
    )
    back = lax.cond(
        is_low,
        lambda later, lower, *parts: later,
        lambda later, lower, *parts: finish(*parts, later[:HALF], lower),
        later,
        lower,
        *parts,
    )
    return pl.pallas_call(
        unpack_kernel,
        out_shape=jax.ShapeDtypeStruct((ROWS, PEERS * DH), bf16),
        in_specs=[VMEM],
        out_specs=VMEM,
        compiler_params=params(),
        name="unpack",
    )(back)


def solution(mesh):
    mesh = Mesh(mesh.devices.reshape(PLANES, GROUPS, LANES), ("z", "g", "x"))
    rows = P(("z", "g", "x"), None)
    return jax.shard_map(
        on_device,
        mesh=mesh,
        in_specs=(rows, rows, rows, P(None, "x"), P(None, "x")),
        out_specs=rows,
        check_vma=False,
    )
```

```python
import math

import jax
import jax.numpy as jnp
from jax import lax
from jax.experimental import pallas as pl
from jax.experimental.pallas import tpu as pltpu
from jax.sharding import Mesh, PartitionSpec as P

DH = 128
BUCKETS = 32
MAXDIST = 128
R1 = 4
R2 = 64
SPAN = 256
PLANES = 16
GROUPS = 8
LANES = 4
PEERS = GROUPS * LANES
ROWS = 32
SEG = PEERS * ROWS
KEPT = SEG // R2
HALF = PLANES // 2
LOW = [6, 0, 1, 2, 3, 4, 5, 7]
HIGH = [11, 8, 9, 10, 12, 13, 14, 15]
ORDER_IN = [(2 * y + c) * LANES + x for c in (1, 0) for y in (3, 2, 1, 0) for x in (3, 2, 1, 0)]
ORDER_OUT = [(2 * y + c) * LANES + x for c in (1, 0) for y in (3, 2, 1, 0) for x in (0, 1, 2, 3)]
PAIRS_IN = [n // 2 for n in ORDER_IN[::2]]
PAIRS_OUT = [n // 2 for n in ORDER_OUT[::2]]
PLACE = {n: p for p, n in enumerate(ORDER_IN)}
UPPER = [12, 13, 14, 15, 11, 10, 8, 9]
NEG = -1e30
SCALE = DH ** (-0.5)

VMEM = pl.BlockSpec(memory_space=pltpu.VMEM)
SMEM = pl.BlockSpec(memory_space=pltpu.SMEM)
HBM = pl.BlockSpec(memory_space=pltpu.HBM)


def params():
    return pltpu.CompilerParams(vmem_limit_bytes=24 * 1024 * 1024)


def bucket_starts():
    half = BUCKETS // 2
    starts = list(range(half + 1))
    for target in range(half + 1, BUCKETS):
        starts.append(int(math.ceil(half * (MAXDIST / half) ** ((target - half) / half))))
    return starts


def pack_kernel(
    q_ref, k_ref, v_ref, offsets_ref, bias_ref, _, out_ref, picks_ref, table_ref, __, sems
):
    copies = [
        pltpu.make_async_copy(offsets_ref, picks_ref, sems.at[3]),
        pltpu.make_async_copy(bias_ref, table_ref, sems.at[4]),
    ]
    for n, ref in enumerate((q_ref, k_ref, v_ref)):
        for g in range(GROUPS):
            for x in range(LANES):
                p, h = PLACE[g * LANES + x], GROUPS * x + g
                copies.append(
                    pltpu.make_async_copy(
                        ref.at[:, h * DH : (h + 1) * DH],
                        out_ref.at[p, n * ROWS : (n + 1) * ROWS],
                        sems.at[n],
                    )
                )
    for copy in copies:
        copy.start()
    for copy in copies:
        copy.wait()


def offset_of(ref, row):
    values = ref[...]
    at_row = lax.broadcasted_iota(jnp.int32, values.shape, 0) == row
    at_head = lax.broadcasted_iota(jnp.int32, values.shape, 1) == lax.axis_index("g")
    return jnp.sum(jnp.where(at_row & at_head, values, 0))


def unpack_kernel(in_ref, out_ref):
    for p, n in enumerate(ORDER_OUT):
        h = GROUPS * (n % LANES) + n // LANES
        out_ref[:, h * DH : (h + 1) * DH] = in_ref[p]


def bias_kernel(table_ref, near_ref, mid_ref, far_ref):
    starts = bucket_starts()
    head = lax.axis_index("g")
    width = 2 * SPAN
    lane = lax.broadcasted_iota(jnp.int32, (8, width), 1)
    steps = jnp.where(lane == 0, 0, width - lane)

    def value_at(distance):
        value = jnp.full(distance.shape, table_ref[head, 0], jnp.float32)
        for n in range(1, BUCKETS):
            value = jnp.where(distance >= starts[n], table_ref[head, n], value)
        return value

    def line(stride):
        return jnp.where((lane == 0) | (lane > SPAN), value_at(steps * stride), NEG)

    def spread(row, count):
        wide = jnp.broadcast_to(row[0:1], (count, width))
        return pltpu.roll(wide, 0, 1, stride=1, stride_axis=0)[:, :SPAN]

    near_ref[...] = spread(line(1), SPAN)
    mid_ref[...] = spread(line(R1), SPAN)
    row = lax.broadcasted_iota(jnp.int32, (KEPT, SPAN), 0)
    column = lax.broadcasted_iota(jnp.int32, (KEPT, SPAN), 1)
    here = lax.axis_index("z")
    plane = jnp.full((KEPT, SPAN), PLANES, jnp.int32)
    for n in range(HALF):
        own = jnp.where(here < HALF, LOW[n], HIGH[n])
        other = jnp.where(here < HALF, PLANES, LOW[n])
        plane = jnp.where(column // KEPT == n, own, plane)
        plane = jnp.where(column // KEPT == n + HALF, other, plane)
    query, key = jnp.zeros((KEPT, SPAN), jnp.int32), jnp.zeros((KEPT, SPAN), jnp.int32)
    for n in range(KEPT):
        query = jnp.where(row == n, PAIRS_OUT[n], query)
        key = jnp.where(column % KEPT == n, PAIRS_IN[n], key)
    apart = (here - plane) * KEPT + query - key
    far_ref[...] = jnp.where(apart >= 0, value_at(apart * R2), NEG)


def kept_tile(ref, part, pick):
    half = pick // ROWS
    within = pick % ROWS
    tile = (within // 16) * 16
    rows = ref[:, 1 - half, pl.ds(pl.multiple_of(part * ROWS + tile, 16), 16), :]
    spot = lax.broadcasted_iota(jnp.int32, (KEPT, 16, DH), 1)
    return jnp.sum(jnp.where(spot == within - tile, rows.astype(jnp.float32), 0.0), axis=1)


def kept_kernel(offsets_ref, qkv_ref, out_ref):
    pick = offset_of(offsets_ref, 1)
    keys = kept_tile(qkv_ref, 1, pick).astype(jnp.bfloat16)
    values = kept_tile(qkv_ref, 2, pick).astype(jnp.bfloat16)
    for z in range(HALF):
        out_ref[z, 0:KEPT] = keys
        out_ref[z, KEPT : 2 * KEPT] = values


def branch(q, k, v, bias):
    scores = lax.dot_general(
        q, k, (((1,), (1,)), ((), ())), preferred_element_type=jnp.float32
    ) * SCALE + bias
    top = jnp.max(scores, axis=1, keepdims=True)
    weight = jnp.exp(scores - top)
    total = jnp.sum(weight, axis=1, keepdims=True)
    acc = jnp.dot(weight.astype(jnp.bfloat16), v, preferred_element_type=jnp.float32)
    shape = acc.shape
    return acc, jnp.broadcast_to(top, shape), jnp.broadcast_to(total, shape)


def merge(one, two):
    acc1, top1, total1 = one
    acc2, top2, total2 = two
    top = jnp.maximum(top1, top2)
    w1, w2 = jnp.exp(top1 - top), jnp.exp(top2 - top)
    return acc1 * w1 + acc2 * w2, top, total1 * w1 + total2 * w2


def local_kernel(
    offsets_ref, qkv_ref, near_ref, mid_ref, out_ref, far_ref, wide, acc_ref, top_ref, total_ref
):
    near_bias = near_ref[...]
    count = SPAN // ROWS
    for s in range(SEG // SPAN):
        blocks = [PLACE[n] for n in range(s * count, (s + 1) * count)]
        rows = slice(s * SPAN, (s + 1) * SPAN)
        q, k, v = (
            jnp.concatenate([qkv_ref[p, n * ROWS : (n + 1) * ROWS] for p in blocks], axis=0)
            for n in range(3)
        )
        wide[0, rows] = q.astype(jnp.float32)
        wide[1, rows] = k.astype(jnp.float32)
        wide[2, rows] = v.astype(jnp.float32)
        acc_ref[rows], top_ref[rows], total_ref[rows] = branch(q, k, v, near_bias)
    kept = pl.ds(offset_of(offsets_ref, 0), SPAN, stride=R1)
    q, k, v = (wide[n, kept, :].astype(jnp.bfloat16) for n in range(3))
    mid = branch(q, k, v, mid_ref[...])
    merged = merge((acc_ref[kept, :], top_ref[kept, :], total_ref[kept, :]), mid)
    acc_ref[kept, :], top_ref[kept, :], total_ref[kept, :] = merged
    for p, n in enumerate(ORDER_OUT):
        rows = slice(n * ROWS, (n + 1) * ROWS)
        out_ref[p] = (acc_ref[rows] / total_ref[rows]).astype(jnp.bfloat16)
    far = pl.ds(offset_of(offsets_ref, 1), KEPT, stride=R2)
    parts = acc_ref[far, :], top_ref[far, :], total_ref[far, :], wide[0, far, :]
    for n, part in enumerate(parts):
        for m, pair in enumerate(PAIRS_OUT):
            far_ref[n, m : m + 1] = part[pair : pair + 1]


def far_kernel(offsets_ref, bias_ref, far_ref, *refs):
    *kv_refs, in_ref, out_ref = refs
    q = far_ref[3].astype(jnp.bfloat16)
    kv = jnp.concatenate([ref[...] for ref in kv_refs], axis=0)
    count = kv.shape[0] * KEPT
    k = kv[:, 0:KEPT].reshape(count, DH)
    v = kv[:, KEPT : 2 * KEPT].reshape(count, DH)
    far = branch(q, k, v, bias_ref[:, 0:count])
    acc, _, total = merge((far_ref[0], far_ref[1], far_ref[2]), far)
    row = (acc / total).astype(jnp.bfloat16).astype(jnp.float32)
    out_ref[...] = in_ref[...]
    pick = offset_of(offsets_ref, 1)
    half = pick // ROWS
    within = pick % ROWS
    tile = (within // 16) * 16
    spot = lax.broadcasted_iota(jnp.int32, (KEPT, 16, DH), 1)
    rows = pl.ds(pl.multiple_of(tile, 16), 16)
    old = in_ref[:, half, rows, :].astype(jnp.float32)
    new = jnp.where(spot == within - tile, jnp.broadcast_to(row[:, None], old.shape), old)
    out_ref[:, half, rows, :] = new.astype(jnp.bfloat16)


def on_device(queries, key_rows, value_rows, rel_bias, offsets):
    bf16, f32 = jnp.bfloat16, jnp.float32
    is_low = lax.axis_index("z") < HALF
    given = (queries, key_rows, value_rows, offsets, rel_bias.T, is_low.astype(jnp.int32)[None])
    packed, picks, table, spare = pl.pallas_call(
        pack_kernel,
        out_shape=(
            jax.ShapeDtypeStruct((PEERS, 3 * ROWS, DH), bf16),
            jax.ShapeDtypeStruct(offsets.shape, offsets.dtype),
            jax.ShapeDtypeStruct(rel_bias.T.shape, f32),
            jax.ShapeDtypeStruct((HALF, 2 * KEPT, DH), bf16),
        ),
        in_specs=[HBM] * 6,
        out_specs=(VMEM, VMEM, VMEM, HBM),
        scratch_shapes=[pltpu.SemaphoreType.DMA((5,))],
        compiler_params=params(),
        name="pack",
    )(*(pltpu.with_memory_space_constraint(t, pltpu.HBM) for t in given))
    qkv = lax.all_to_all(packed, ("g", "x"), 0, 0, axis_index_groups=[ORDER_IN], tiled=True)
    kept = pl.pallas_call(
        kept_kernel,
        out_shape=jax.ShapeDtypeStruct((HALF, 2 * KEPT, DH), bf16),
        in_specs=[VMEM, VMEM],
        out_specs=VMEM,
        compiler_params=params(),
        name="kept",
    )(picks, qkv.reshape(KEPT, 2, 3 * ROWS, DH))
    def exchange(block):
        return lax.all_to_all(block, "z", 0, 0, axis_index_groups=[LOW, HIGH], tiled=True)

    def local(qkv, table):
        near_bias, mid_bias, far_bias = pl.pallas_call(
            bias_kernel,
            out_shape=(
                jax.ShapeDtypeStruct((SPAN, SPAN), f32),
                jax.ShapeDtypeStruct((SPAN, SPAN), f32),
                jax.ShapeDtypeStruct((KEPT, SPAN), f32),
            ),
            in_specs=[SMEM],
            out_specs=(VMEM, VMEM, VMEM),
            compiler_params=params(),
            name="bias",
        )(table)
        rows, far_parts = pl.pallas_call(
            local_kernel,
            out_shape=(
                jax.ShapeDtypeStruct((PEERS, ROWS, DH), bf16),
                jax.ShapeDtypeStruct((4, KEPT, DH), f32),
            ),
            in_specs=[VMEM] * 4,
            out_specs=(VMEM, VMEM),
            scratch_shapes=[
                pltpu.VMEM((3, SEG, DH), f32),
                pltpu.VMEM((SEG, DH), f32),
                pltpu.VMEM((SEG, DH), f32),
                pltpu.VMEM((SEG, DH), f32),
            ],
            compiler_params=params(),
            name="local",
        )(picks, qkv, near_bias, mid_bias)
        return rows, far_parts, far_bias

    def finish(rows, far_parts, far_bias, *kv):
        merged = pl.pallas_call(
            far_kernel,
            out_shape=jax.ShapeDtypeStruct((KEPT, 2, ROWS, DH), bf16),
            in_specs=[VMEM] * (4 + len(kv)),
            out_specs=VMEM,
            input_output_aliases={3 + len(kv): 0},
            compiler_params=params(),
            name="far",
        )(picks, far_bias, far_parts, *kv, rows.reshape(KEPT, 2, ROWS, DH))
        return lax.all_to_all(
            merged.reshape(PEERS, ROWS, DH),
            ("g", "x"),
            0,
            0,
            axis_index_groups=[ORDER_OUT],
            tiled=True,
        )

    first, *parts = lax.cond(
        is_low,
        lambda block, spare, *rest: (exchange(block), *local(*rest)),
        lambda block, spare, *rest: (spare, *local(*rest)),
        kept,
        spare,
        qkv,
        table,
    )
    lower = lax.ppermute(first, "z", list(enumerate(UPPER)))
    later = lax.cond(
        is_low,
        lambda first, kept, *parts: finish(*parts, first),
        lambda first, kept, *parts: jnp.pad(exchange(kept), ((0, PEERS - HALF), (0, 0), (0, 0))),
        first,
        kept,
        *parts,
    )
    back = lax.cond(
        is_low,
        lambda later, lower, *parts: later,
        lambda later, lower, *parts: finish(*parts, later[:HALF], lower),
        later,
        lower,
        *parts,
    )
    return pl.pallas_call(
        unpack_kernel,
        out_shape=jax.ShapeDtypeStruct((ROWS, PEERS * DH), bf16),
        in_specs=[VMEM],
        out_specs=VMEM,
        compiler_params=params(),
        name="unpack",
    )(back)


def solution(mesh):
    mesh = Mesh(mesh.devices.reshape(PLANES, GROUPS, LANES), ("z", "g", "x"))
    rows = P(("z", "g", "x"), None)
    return jax.shard_map(
        on_device,
        mesh=mesh,
        in_specs=(rows, rows, rows, P(None, "x"), P(None, "x")),
        out_specs=rows,
        check_vma=False,
    )
```

```python
import math

import jax
import jax.numpy as jnp
from jax import lax
from jax.experimental import pallas as pl
from jax.experimental.pallas import tpu as pltpu
from jax.sharding import Mesh, PartitionSpec as P

DH = 128
BUCKETS = 32
MAXDIST = 128
R1 = 4
R2 = 64
SPAN = 256
PLANES = 16
GROUPS = 8
LANES = 4
PEERS = GROUPS * LANES
ROWS = 32
SEG = PEERS * ROWS
KEPT = SEG // R2
HALF = PLANES // 2
LOW = [6, 0, 1, 2, 3, 4, 5, 7]
HIGH = [11, 8, 9, 10, 12, 13, 14, 15]
ORDER_IN = [(2 * y + c) * LANES + x for c in (1, 0) for y in (3, 2, 1, 0) for x in (3, 2, 1, 0)]
ORDER_OUT = [(2 * y + c) * LANES + x for c in (1, 0) for y in (3, 2, 1, 0) for x in (0, 1, 2, 3)]
PAIRS_IN = [n // 2 for n in ORDER_IN[::2]]
PAIRS_OUT = [n // 2 for n in ORDER_OUT[::2]]
PLACE = {n: p for p, n in enumerate(ORDER_IN)}
UPPER = [12, 13, 14, 15, 11, 9, 10, 8]
NEG = -1e30
SCALE = DH ** (-0.5)

VMEM = pl.BlockSpec(memory_space=pltpu.VMEM)
SMEM = pl.BlockSpec(memory_space=pltpu.SMEM)
HBM = pl.BlockSpec(memory_space=pltpu.HBM)


def params():
    return pltpu.CompilerParams(vmem_limit_bytes=24 * 1024 * 1024)


def bucket_starts():
    half = BUCKETS // 2
    starts = list(range(half + 1))
    for target in range(half + 1, BUCKETS):
        starts.append(int(math.ceil(half * (MAXDIST / half) ** ((target - half) / half))))
    return starts


def pack_kernel(
    q_ref, k_ref, v_ref, offsets_ref, bias_ref, _, out_ref, picks_ref, table_ref, __, sems
):
    copies = [
        pltpu.make_async_copy(offsets_ref, picks_ref, sems.at[3]),
        pltpu.make_async_copy(bias_ref, table_ref, sems.at[4]),
    ]
    for n, ref in enumerate((q_ref, k_ref, v_ref)):
        for g in range(GROUPS):
            for x in range(LANES):
                p, h = PLACE[g * LANES + x], GROUPS * x + g
                copies.append(
                    pltpu.make_async_copy(
                        ref.at[:, h * DH : (h + 1) * DH],
                        out_ref.at[p, n * ROWS : (n + 1) * ROWS],
                        sems.at[n],
                    )
                )
    for copy in copies:
        copy.start()
    for copy in copies:
        copy.wait()


def offset_of(ref, row):
    values = ref[...]
    at_row = lax.broadcasted_iota(jnp.int32, values.shape, 0) == row
    at_head = lax.broadcasted_iota(jnp.int32, values.shape, 1) == lax.axis_index("g")
    return jnp.sum(jnp.where(at_row & at_head, values, 0))


def unpack_kernel(in_ref, out_ref, block, sems):
    copies = []
    for x in range(LANES):
        for g in range(GROUPS):
            h = GROUPS * x + g
            block[:, h * DH : (h + 1) * DH] = in_ref[ORDER_OUT.index(g * LANES + x)]
        columns = slice(x * GROUPS * DH, (x + 1) * GROUPS * DH)
        copies.append(pltpu.make_async_copy(block.at[:, columns], out_ref.at[:, columns], sems.at[x]))
        copies[-1].start()
    for copy in copies:
        copy.wait()


def bias_kernel(table_ref, near_ref, mid_ref, far_ref):
    starts = bucket_starts()
    head = lax.axis_index("g")
    width = 2 * SPAN
    lane = lax.broadcasted_iota(jnp.int32, (8, width), 1)
    steps = jnp.where(lane == 0, 0, width - lane)

    def value_at(distance):
        value = jnp.full(distance.shape, table_ref[head, 0], jnp.float32)
        for n in range(1, BUCKETS):
            value = jnp.where(distance >= starts[n], table_ref[head, n], value)
        return value

    def line(stride):
        return jnp.where((lane == 0) | (lane > SPAN), value_at(steps * stride), NEG)

    def spread(row, count):
        wide = jnp.broadcast_to(row[0:1], (count, width))
        return pltpu.roll(wide, 0, 1, stride=1, stride_axis=0)[:, :SPAN]

    near_ref[...] = spread(line(1), SPAN)
    mid_ref[...] = spread(line(R1), SPAN)
    row = lax.broadcasted_iota(jnp.int32, (KEPT, SPAN), 0)
    column = lax.broadcasted_iota(jnp.int32, (KEPT, SPAN), 1)
    here = lax.axis_index("z")
    plane = jnp.full((KEPT, SPAN), PLANES, jnp.int32)
    for n in range(HALF):
        own = jnp.where(here < HALF, LOW[n], HIGH[n])
        other = jnp.where(here < HALF, PLANES, LOW[n])
        plane = jnp.where(column // KEPT == n, own, plane)
        plane = jnp.where(column // KEPT == n + HALF, other, plane)
    query, key = jnp.zeros((KEPT, SPAN), jnp.int32), jnp.zeros((KEPT, SPAN), jnp.int32)
    for n in range(KEPT):
        query = jnp.where(row == n, PAIRS_OUT[n], query)
        key = jnp.where(column % KEPT == n, PAIRS_IN[n], key)
    apart = (here - plane) * KEPT + query - key
    far_ref[...] = jnp.where(apart >= 0, value_at(apart * R2), NEG)


def kept_tile(ref, part, pick):
    half = pick // ROWS
    within = pick % ROWS
    tile = (within // 16) * 16
    rows = ref[:, 1 - half, pl.ds(pl.multiple_of(part * ROWS + tile, 16), 16), :]
    spot = lax.broadcasted_iota(jnp.int32, (KEPT, 16, DH), 1)
    return jnp.sum(jnp.where(spot == within - tile, rows.astype(jnp.float32), 0.0), axis=1)


def kept_kernel(offsets_ref, qkv_ref, out_ref):
    pick = offset_of(offsets_ref, 1)
    keys = kept_tile(qkv_ref, 1, pick).astype(jnp.bfloat16)
    values = kept_tile(qkv_ref, 2, pick).astype(jnp.bfloat16)
    for z in range(HALF):
        out_ref[z, 0:KEPT] = keys
        out_ref[z, KEPT : 2 * KEPT] = values


def branch(q, k, v, bias):
    scores = lax.dot_general(
        q, k, (((1,), (1,)), ((), ())), preferred_element_type=jnp.float32
    ) * SCALE + bias
    top = jnp.max(scores, axis=1, keepdims=True)
    weight = jnp.exp(scores - top)
    total = jnp.sum(weight, axis=1, keepdims=True)
    acc = jnp.dot(weight.astype(jnp.bfloat16), v, preferred_element_type=jnp.float32)
    shape = acc.shape
    return acc, jnp.broadcast_to(top, shape), jnp.broadcast_to(total, shape)


def merge(one, two):
    acc1, top1, total1 = one
    acc2, top2, total2 = two
    top = jnp.maximum(top1, top2)
    w1, w2 = jnp.exp(top1 - top), jnp.exp(top2 - top)
    return acc1 * w1 + acc2 * w2, top, total1 * w1 + total2 * w2


def local_kernel(
    offsets_ref, qkv_ref, near_ref, mid_ref, out_ref, far_ref, wide, acc_ref, top_ref, total_ref
):
    near_bias = near_ref[...]
    count = SPAN // ROWS
    for s in range(SEG // SPAN):
        blocks = [PLACE[n] for n in range(s * count, (s + 1) * count)]
        rows = slice(s * SPAN, (s + 1) * SPAN)
        q, k, v = (
            jnp.concatenate([qkv_ref[p, n * ROWS : (n + 1) * ROWS] for p in blocks], axis=0)
            for n in range(3)
        )
        wide[0, rows] = q.astype(jnp.float32)
        wide[1, rows] = k.astype(jnp.float32)
        wide[2, rows] = v.astype(jnp.float32)
        acc_ref[rows], top_ref[rows], total_ref[rows] = branch(q, k, v, near_bias)
    kept = pl.ds(offset_of(offsets_ref, 0), SPAN, stride=R1)
    q, k, v = (wide[n, kept, :].astype(jnp.bfloat16) for n in range(3))
    mid = branch(q, k, v, mid_ref[...])
    merged = merge((acc_ref[kept, :], top_ref[kept, :], total_ref[kept, :]), mid)
    acc_ref[kept, :], top_ref[kept, :], total_ref[kept, :] = merged
    for p, n in enumerate(ORDER_OUT):
        rows = slice(n * ROWS, (n + 1) * ROWS)
        out_ref[p] = (acc_ref[rows] / total_ref[rows]).astype(jnp.bfloat16)
    far = pl.ds(offset_of(offsets_ref, 1), KEPT, stride=R2)
    parts = acc_ref[far, :], top_ref[far, :], total_ref[far, :], wide[0, far, :]
    for n, part in enumerate(parts):
        for m, pair in enumerate(PAIRS_OUT):
            far_ref[n, m : m + 1] = part[pair : pair + 1]


def far_kernel(offsets_ref, bias_ref, far_ref, *refs):
    *kv_refs, in_ref, out_ref = refs
    q = far_ref[3].astype(jnp.bfloat16)
    kv = jnp.concatenate([ref[...] for ref in kv_refs], axis=0)
    count = kv.shape[0] * KEPT
    k = kv[:, 0:KEPT].reshape(count, DH)
    v = kv[:, KEPT : 2 * KEPT].reshape(count, DH)
    far = branch(q, k, v, bias_ref[:, 0:count])
    acc, _, total = merge((far_ref[0], far_ref[1], far_ref[2]), far)
    row = (acc / total).astype(jnp.bfloat16).astype(jnp.float32)
    out_ref[...] = in_ref[...]
    pick = offset_of(offsets_ref, 1)
    half = pick // ROWS
    within = pick % ROWS
    tile = (within // 16) * 16
    spot = lax.broadcasted_iota(jnp.int32, (KEPT, 16, DH), 1)
    rows = pl.ds(pl.multiple_of(tile, 16), 16)
    old = in_ref[:, half, rows, :].astype(jnp.float32)
    new = jnp.where(spot == within - tile, jnp.broadcast_to(row[:, None], old.shape), old)
    out_ref[:, half, rows, :] = new.astype(jnp.bfloat16)


def on_device(queries, key_rows, value_rows, rel_bias, offsets):
    bf16, f32 = jnp.bfloat16, jnp.float32
    is_low = lax.axis_index("z") < HALF
    given = (queries, key_rows, value_rows, offsets, rel_bias.T, is_low.astype(jnp.int32)[None])
    packed, picks, table, spare = pl.pallas_call(
        pack_kernel,
        out_shape=(
            jax.ShapeDtypeStruct((PEERS, 3 * ROWS, DH), bf16),
            jax.ShapeDtypeStruct(offsets.shape, offsets.dtype),
            jax.ShapeDtypeStruct(rel_bias.T.shape, f32),
            jax.ShapeDtypeStruct((HALF, 2 * KEPT, DH), bf16),
        ),
        in_specs=[HBM] * 6,
        out_specs=(VMEM, VMEM, VMEM, HBM),
        scratch_shapes=[pltpu.SemaphoreType.DMA((5,))],
        compiler_params=params(),
        name="pack",
    )(*(pltpu.with_memory_space_constraint(t, pltpu.HBM) for t in given))
    qkv = lax.all_to_all(packed, ("g", "x"), 0, 0, axis_index_groups=[ORDER_IN], tiled=True)
    kept = pl.pallas_call(
        kept_kernel,
        out_shape=jax.ShapeDtypeStruct((HALF, 2 * KEPT, DH), bf16),
        in_specs=[VMEM, VMEM],
        out_specs=VMEM,
        compiler_params=params(),
        name="kept",
    )(picks, qkv.reshape(KEPT, 2, 3 * ROWS, DH))
    def exchange(block):
        return lax.all_to_all(block, "z", 0, 0, axis_index_groups=[LOW, HIGH], tiled=True)

    def local(qkv, table):
        near_bias, mid_bias, far_bias = pl.pallas_call(
            bias_kernel,
            out_shape=(
                jax.ShapeDtypeStruct((SPAN, SPAN), f32),
                jax.ShapeDtypeStruct((SPAN, SPAN), f32),
                jax.ShapeDtypeStruct((KEPT, SPAN), f32),
            ),
            in_specs=[SMEM],
            out_specs=(VMEM, VMEM, VMEM),
            compiler_params=params(),
            name="bias",
        )(table)
        rows, far_parts = pl.pallas_call(
            local_kernel,
            out_shape=(
                jax.ShapeDtypeStruct((PEERS, ROWS, DH), bf16),
                jax.ShapeDtypeStruct((4, KEPT, DH), f32),
            ),
            in_specs=[VMEM] * 4,
            out_specs=(VMEM, VMEM),
            scratch_shapes=[
                pltpu.VMEM((3, SEG, DH), f32),
                pltpu.VMEM((SEG, DH), f32),
                pltpu.VMEM((SEG, DH), f32),
                pltpu.VMEM((SEG, DH), f32),
            ],
            compiler_params=params(),
            name="local",
        )(picks, qkv, near_bias, mid_bias)
        return rows, far_parts, far_bias

    def finish(rows, far_parts, far_bias, *kv):
        merged = pl.pallas_call(
            far_kernel,
            out_shape=jax.ShapeDtypeStruct((KEPT, 2, ROWS, DH), bf16),
            in_specs=[VMEM] * (4 + len(kv)),
            out_specs=VMEM,
            input_output_aliases={3 + len(kv): 0},
            compiler_params=params(),
            name="far",
        )(picks, far_bias, far_parts, *kv, rows.reshape(KEPT, 2, ROWS, DH))
        return lax.all_to_all(
            merged.reshape(PEERS, ROWS, DH),
            ("g", "x"),
            0,
            0,
            axis_index_groups=[ORDER_OUT],
            tiled=True,
        )

    first, *parts = lax.cond(
        is_low,
        lambda block, spare, *rest: (exchange(block), *local(*rest)),
        lambda block, spare, *rest: (spare, *local(*rest)),
        kept,
        spare,
        qkv,
        table,
    )
    lower = lax.ppermute(first, "z", list(enumerate(UPPER)))
    later = lax.cond(
        is_low,
        lambda first, kept, *parts: finish(*parts, first),
        lambda first, kept, *parts: jnp.pad(exchange(kept), ((0, PEERS - HALF), (0, 0), (0, 0))),
        first,
        kept,
        *parts,
    )
    back = lax.cond(
        is_low,
        lambda later, lower, *parts: later,
        lambda later, lower, *parts: finish(*parts, later[:HALF], lower),
        later,
        lower,
        *parts,
    )
    return pl.pallas_call(
        unpack_kernel,
        out_shape=jax.ShapeDtypeStruct((ROWS, PEERS * DH), bf16),
        in_specs=[VMEM],
        out_specs=HBM,
        scratch_shapes=[
            pltpu.VMEM((ROWS, PEERS * DH), bf16),
            pltpu.SemaphoreType.DMA((LANES,)),
        ],
        compiler_params=params(),
        name="unpack",
    )(back)


def solution(mesh):
    mesh = Mesh(mesh.devices.reshape(PLANES, GROUPS, LANES), ("z", "g", "x"))
    rows = P(("z", "g", "x"), None)
    return jax.shard_map(
        on_device,
        mesh=mesh,
        in_specs=(rows, rows, rows, P(None, "x"), P(None, "x")),
        out_specs=rows,
        check_vma=False,
    )
```

```python
import math

import jax
import jax.numpy as jnp
from jax import lax
from jax.experimental import pallas as pl
from jax.experimental.pallas import tpu as pltpu
from jax.sharding import Mesh, PartitionSpec as P

DH = 128
BUCKETS = 32
MAXDIST = 128
R1 = 4
R2 = 64
SPAN = 256
PLANES = 16
GROUPS = 8
LANES = 4
PEERS = GROUPS * LANES
ROWS = 32
SEG = PEERS * ROWS
KEPT = SEG // R2
HALF = PLANES // 2
LOW = [6, 0, 1, 2, 3, 4, 5, 7]
HIGH = [10, 8, 9, 11, 12, 13, 14, 15]
ORDER_IN = [(2 * y + c) * LANES + x for c in (1, 0) for y in (3, 2, 1, 0) for x in (3, 2, 1, 0)]
ORDER_OUT = [(2 * y + c) * LANES + x for c in (1, 0) for y in (3, 2, 1, 0) for x in (0, 1, 2, 3)]
PAIRS_IN = [n // 2 for n in ORDER_IN[::2]]
PAIRS_OUT = [n // 2 for n in ORDER_OUT[::2]]
PLACE = {n: p for p, n in enumerate(ORDER_IN)}
UPPER = [12, 13, 14, 15, 11, 10, 8, 9]
NEG = -1e30
SCALE = DH ** (-0.5)

VMEM = pl.BlockSpec(memory_space=pltpu.VMEM)
SMEM = pl.BlockSpec(memory_space=pltpu.SMEM)
HBM = pl.BlockSpec(memory_space=pltpu.HBM)


def params():
    return pltpu.CompilerParams(vmem_limit_bytes=24 * 1024 * 1024)


def bucket_starts():
    half = BUCKETS // 2
    starts = list(range(half + 1))
    for target in range(half + 1, BUCKETS):
        starts.append(int(math.ceil(half * (MAXDIST / half) ** ((target - half) / half))))
    return starts


def pack_kernel(
    q_ref, k_ref, v_ref, offsets_ref, bias_ref, _, out_ref, picks_ref, table_ref, __, sems
):
    copies = [
        pltpu.make_async_copy(offsets_ref, picks_ref, sems.at[3]),
        pltpu.make_async_copy(bias_ref, table_ref, sems.at[4]),
    ]
    for n, ref in enumerate((q_ref, k_ref, v_ref)):
        for g in range(GROUPS):
            for x in range(LANES):
                p, h = PLACE[g * LANES + x], GROUPS * x + g
                copies.append(
                    pltpu.make_async_copy(
                        ref.at[:, h * DH : (h + 1) * DH],
                        out_ref.at[p, n * ROWS : (n + 1) * ROWS],
                        sems.at[n],
                    )
                )
    for copy in copies:
        copy.start()
    for copy in copies:
        copy.wait()


def offset_of(ref, row):
    values = ref[...]
    at_row = lax.broadcasted_iota(jnp.int32, values.shape, 0) == row
    at_head = lax.broadcasted_iota(jnp.int32, values.shape, 1) == lax.axis_index("g")
    return jnp.sum(jnp.where(at_row & at_head, values, 0))


def unpack_kernel(in_ref, out_ref):
    for p, n in enumerate(ORDER_OUT):
        h = GROUPS * (n % LANES) + n // LANES
        out_ref[:, h * DH : (h + 1) * DH] = in_ref[p]


def bias_kernel(table_ref, near_ref, mid_ref, far_ref):
    starts = bucket_starts()
    head = lax.axis_index("g")
    width = 2 * SPAN
    lane = lax.broadcasted_iota(jnp.int32, (8, width), 1)
    steps = jnp.where(lane == 0, 0, width - lane)

    def value_at(distance):
        value = jnp.full(distance.shape, table_ref[head, 0], jnp.float32)
        for n in range(1, BUCKETS):
            value = jnp.where(distance >= starts[n], table_ref[head, n], value)
        return value

    def line(stride):
        return jnp.where((lane == 0) | (lane > SPAN), value_at(steps * stride), NEG)

    def spread(row, count):
        wide = jnp.broadcast_to(row[0:1], (count, width))
        return pltpu.roll(wide, 0, 1, stride=1, stride_axis=0)[:, :SPAN]

    near_ref[...] = spread(line(1), SPAN)
    mid_ref[...] = spread(line(R1), SPAN)
    row = lax.broadcasted_iota(jnp.int32, (KEPT, SPAN), 0)
    column = lax.broadcasted_iota(jnp.int32, (KEPT, SPAN), 1)
    here = lax.axis_index("z")
    plane = jnp.full((KEPT, SPAN), PLANES, jnp.int32)
    for n in range(HALF):
        own = jnp.where(here < HALF, LOW[n], HIGH[n])
        other = jnp.where(here < HALF, PLANES, LOW[n])
        plane = jnp.where(column // KEPT == n, own, plane)
        plane = jnp.where(column // KEPT == n + HALF, other, plane)
    query, key = jnp.zeros((KEPT, SPAN), jnp.int32), jnp.zeros((KEPT, SPAN), jnp.int32)
    for n in range(KEPT):
        query = jnp.where(row == n, PAIRS_OUT[n], query)
        key = jnp.where(column % KEPT == n, PAIRS_IN[n], key)
    apart = (here - plane) * KEPT + query - key
    far_ref[...] = jnp.where(apart >= 0, value_at(apart * R2), NEG)


def kept_tile(ref, part, pick):
    half = pick // ROWS
    within = pick % ROWS
    tile = (within // 16) * 16
    rows = ref[:, 1 - half, pl.ds(pl.multiple_of(part * ROWS + tile, 16), 16), :]
    spot = lax.broadcasted_iota(jnp.int32, (KEPT, 16, DH), 1)
    return jnp.sum(jnp.where(spot == within - tile, rows.astype(jnp.float32), 0.0), axis=1)


def kept_kernel(offsets_ref, qkv_ref, out_ref):
    pick = offset_of(offsets_ref, 1)
    keys = kept_tile(qkv_ref, 1, pick).astype(jnp.bfloat16)
    values = kept_tile(qkv_ref, 2, pick).astype(jnp.bfloat16)
    for z in range(HALF):
        out_ref[z, 0:KEPT] = keys
        out_ref[z, KEPT : 2 * KEPT] = values


def branch(q, k, v, bias):
    scores = lax.dot_general(
        q, k, (((1,), (1,)), ((), ())), preferred_element_type=jnp.float32
    ) * SCALE + bias
    top = jnp.max(scores, axis=1, keepdims=True)
    weight = jnp.exp(scores - top)
    total = jnp.sum(weight, axis=1, keepdims=True)
    acc = jnp.dot(weight.astype(jnp.bfloat16), v, preferred_element_type=jnp.float32)
    shape = acc.shape
    return acc, jnp.broadcast_to(top, shape), jnp.broadcast_to(total, shape)


def merge(one, two):
    acc1, top1, total1 = one
    acc2, top2, total2 = two
    top = jnp.maximum(top1, top2)
    w1, w2 = jnp.exp(top1 - top), jnp.exp(top2 - top)
    return acc1 * w1 + acc2 * w2, top, total1 * w1 + total2 * w2


def local_kernel(
    offsets_ref, qkv_ref, near_ref, mid_ref, out_ref, far_ref, wide, acc_ref, top_ref, total_ref
):
    near_bias = near_ref[...]
    count = SPAN // ROWS
    for s in range(SEG // SPAN):
        blocks = [PLACE[n] for n in range(s * count, (s + 1) * count)]
        rows = slice(s * SPAN, (s + 1) * SPAN)
        q, k, v = (
            jnp.concatenate([qkv_ref[p, n * ROWS : (n + 1) * ROWS] for p in blocks], axis=0)
            for n in range(3)
        )
        wide[0, rows] = q.astype(jnp.float32)
        wide[1, rows] = k.astype(jnp.float32)
        wide[2, rows] = v.astype(jnp.float32)
        acc_ref[rows], top_ref[rows], total_ref[rows] = branch(q, k, v, near_bias)
    kept = pl.ds(offset_of(offsets_ref, 0), SPAN, stride=R1)
    q, k, v = (wide[n, kept, :].astype(jnp.bfloat16) for n in range(3))
    mid = branch(q, k, v, mid_ref[...])
    merged = merge((acc_ref[kept, :], top_ref[kept, :], total_ref[kept, :]), mid)
    acc_ref[kept, :], top_ref[kept, :], total_ref[kept, :] = merged
    for p, n in enumerate(ORDER_OUT):
        rows = slice(n * ROWS, (n + 1) * ROWS)
        out_ref[p] = (acc_ref[rows] / total_ref[rows]).astype(jnp.bfloat16)
    far = pl.ds(offset_of(offsets_ref, 1), KEPT, stride=R2)
    parts = acc_ref[far, :], top_ref[far, :], total_ref[far, :], wide[0, far, :]
    for n, part in enumerate(parts):
        for m, pair in enumerate(PAIRS_OUT):
            far_ref[n, m : m + 1] = part[pair : pair + 1]


def far_kernel(offsets_ref, bias_ref, far_ref, *refs):
    *kv_refs, in_ref, out_ref = refs
    q = far_ref[3].astype(jnp.bfloat16)
    kv = jnp.concatenate([ref[...] for ref in kv_refs], axis=0)
    count = kv.shape[0] * KEPT
    k = kv[:, 0:KEPT].reshape(count, DH)
    v = kv[:, KEPT : 2 * KEPT].reshape(count, DH)
    far = branch(q, k, v, bias_ref[:, 0:count])
    acc, _, total = merge((far_ref[0], far_ref[1], far_ref[2]), far)
    row = (acc / total).astype(jnp.bfloat16).astype(jnp.float32)
    out_ref[...] = in_ref[...]
    pick = offset_of(offsets_ref, 1)
    half = pick // ROWS
    within = pick % ROWS
    tile = (within // 16) * 16
    spot = lax.broadcasted_iota(jnp.int32, (KEPT, 16, DH), 1)
    rows = pl.ds(pl.multiple_of(tile, 16), 16)
    old = in_ref[:, half, rows, :].astype(jnp.float32)
    new = jnp.where(spot == within - tile, jnp.broadcast_to(row[:, None], old.shape), old)
    out_ref[:, half, rows, :] = new.astype(jnp.bfloat16)


def on_device(queries, key_rows, value_rows, rel_bias, offsets):
    bf16, f32 = jnp.bfloat16, jnp.float32
    is_low = lax.axis_index("z") < HALF
    given = (queries, key_rows, value_rows, offsets, rel_bias.T, is_low.astype(jnp.int32)[None])
    packed, picks, table, spare = pl.pallas_call(
        pack_kernel,
        out_shape=(
            jax.ShapeDtypeStruct((PEERS, 3 * ROWS, DH), bf16),
            jax.ShapeDtypeStruct(offsets.shape, offsets.dtype),
            jax.ShapeDtypeStruct(rel_bias.T.shape, f32),
            jax.ShapeDtypeStruct((HALF, 2 * KEPT, DH), bf16),
        ),
        in_specs=[HBM] * 6,
        out_specs=(VMEM, VMEM, VMEM, HBM),
        scratch_shapes=[pltpu.SemaphoreType.DMA((5,))],
        compiler_params=params(),
        name="pack",
    )(*(pltpu.with_memory_space_constraint(t, pltpu.HBM) for t in given))
    qkv = lax.all_to_all(packed, ("g", "x"), 0, 0, axis_index_groups=[ORDER_IN], tiled=True)
    kept = pl.pallas_call(
        kept_kernel,
        out_shape=jax.ShapeDtypeStruct((HALF, 2 * KEPT, DH), bf16),
        in_specs=[VMEM, VMEM],
        out_specs=VMEM,
        compiler_params=params(),
        name="kept",
    )(picks, qkv.reshape(KEPT, 2, 3 * ROWS, DH))
    def exchange(block):
        return lax.all_to_all(block, "z", 0, 0, axis_index_groups=[LOW, HIGH], tiled=True)

    def local(qkv, table):
        near_bias, mid_bias, far_bias = pl.pallas_call(
            bias_kernel,
            out_shape=(
                jax.ShapeDtypeStruct((SPAN, SPAN), f32),
                jax.ShapeDtypeStruct((SPAN, SPAN), f32),
                jax.ShapeDtypeStruct((KEPT, SPAN), f32),
            ),
            in_specs=[SMEM],
            out_specs=(VMEM, VMEM, VMEM),
            compiler_params=params(),
            name="bias",
        )(table)
        rows, far_parts = pl.pallas_call(
            local_kernel,
            out_shape=(
                jax.ShapeDtypeStruct((PEERS, ROWS, DH), bf16),
                jax.ShapeDtypeStruct((4, KEPT, DH), f32),
            ),
            in_specs=[VMEM] * 4,
            out_specs=(VMEM, VMEM),
            scratch_shapes=[
                pltpu.VMEM((3, SEG, DH), f32),
                pltpu.VMEM((SEG, DH), f32),
                pltpu.VMEM((SEG, DH), f32),
                pltpu.VMEM((SEG, DH), f32),
            ],
            compiler_params=params(),
            name="local",
        )(picks, qkv, near_bias, mid_bias)
        return rows, far_parts, far_bias

    def finish(rows, far_parts, far_bias, *kv):
        merged = pl.pallas_call(
            far_kernel,
            out_shape=jax.ShapeDtypeStruct((KEPT, 2, ROWS, DH), bf16),
            in_specs=[VMEM] * (4 + len(kv)),
            out_specs=VMEM,
            input_output_aliases={3 + len(kv): 0},
            compiler_params=params(),
            name="far",
        )(picks, far_bias, far_parts, *kv, rows.reshape(KEPT, 2, ROWS, DH))
        return lax.all_to_all(
            merged.reshape(PEERS, ROWS, DH),
            ("g", "x"),
            0,
            0,
            axis_index_groups=[ORDER_OUT],
            tiled=True,
        )

    first, *parts = lax.cond(
        is_low,
        lambda block, spare, *rest: (exchange(block), *local(*rest)),
        lambda block, spare, *rest: (spare, *local(*rest)),
        kept,
        spare,
        qkv,
        table,
    )
    lower = lax.ppermute(first, "z", list(enumerate(UPPER)))
    later = lax.cond(
        is_low,
        lambda first, kept, *parts: finish(*parts, first),
        lambda first, kept, *parts: jnp.pad(exchange(kept), ((0, PEERS - HALF), (0, 0), (0, 0))),
        first,
        kept,
        *parts,
    )
    back = lax.cond(
        is_low,
        lambda later, lower, *parts: later,
        lambda later, lower, *parts: finish(*parts, later[:HALF], lower),
        later,
        lower,
        *parts,
    )
    return pl.pallas_call(
        unpack_kernel,
        out_shape=jax.ShapeDtypeStruct((ROWS, PEERS * DH), bf16),
        in_specs=[VMEM],
        out_specs=VMEM,
        compiler_params=params(),
        name="unpack",
    )(back)


def solution(mesh):
    mesh = Mesh(mesh.devices.reshape(PLANES, GROUPS, LANES), ("z", "g", "x"))
    rows = P(("z", "g", "x"), None)
    return jax.shard_map(
        on_device,
        mesh=mesh,
        in_specs=(rows, rows, rows, P(None, "x"), P(None, "x")),
        out_specs=rows,
        check_vma=False,
    )
```
